128 devices in a mesh: lat: 4 (over z), lon: 32 (over x, y, core).
Axes of the slice: x: 4, y: 4, z: 4, core: 2. Of those that a mesh axis runs over, the one named last changes fastest.
Arguments:
- obs_tiles: bfloat16 [128, 128, 4, 8, 256], P(('lat', 'lon'))
- tile_block: int32 [128, 128, 4], P(('lat', 'lon')), may hold values from 0 to 11
- tile_rows: int32 [128, 128, 4], P(('lat', 'lon')), may hold values from 0 to 256, as said below
- embed_weight: bfloat16 [6, 23], replicated, may hold values from -2.5 to 2.5
- conv1_weight: bfloat16 [9, 24, 256], replicated, may hold values from -0.4375 to 0.4375
- conv1_bias: float32 [256], replicated, may hold values from -3 to 3
- conv2_weight: bfloat16 [9, 256, 512], replicated, may hold values from -0.125 to 0.125
- conv2_bias: float32 [512], replicated, may hold values from -3 to 3
Outputs:
- coarse: bfloat16 [64, 384, 512], P('lat')
The draws below stay inside these ranges and needn't reach their ends.
Inputs may be any that keep to these rules, and one draw needn't show every extreme that they name: `tile_rows`: for each source and destination the live slots come first: all hold 256 rows but the last live one, which holds 1 to 256; later slots hold 0. In every draw one destination block receives 4 live tiles from every source.
All inputs are finite; a program needn't handle non-finite values.
Results may differ from the reference program's by a relative error of at most 0.0052.
Values may be sent and summed in bfloat16 or wider, within the bound.
No kernel may reach another device: no remote copies, remote signals or barrier semaphores. Data moves between devices by JAX's collectives and lax.ppermute only.
A program may use at most 64 MiB of HBM per device.

```python
import jax
import jax.numpy as jnp
from jax import lax

BX = 64
BY = 48
SB = 16
TILE = 256
CAP = 4
FEAT = 8
CH0 = 24
C1 = 256
C2 = 512
BLOCKS = 128
SUBS = 12
NX = 256
NY = 1536
N_LAT = 4
N_LON = 32


def draw_tile_rows(key, part):
    draw_keys = jax.random.split(key, 4)
    ceiling = jax.random.randint(draw_keys[0], (BLOCKS,), CAP // 2, CAP + 1)
    live_tiles = jax.random.randint(draw_keys[1], (BLOCKS, BLOCKS), 0, ceiling[None, :] + 1)
    dense_dest = jax.random.randint(draw_keys[2], (), 0, BLOCKS)
    target = jnp.arange(BLOCKS, dtype=jnp.int32)[None, :]
    live_tiles = jnp.where(target == dense_dest, CAP, live_tiles)
    last_fill = jax.random.randint(draw_keys[3], (BLOCKS, BLOCKS), 1, TILE + 1)
    slot_ids = jnp.arange(CAP, dtype=jnp.int32)[None, None, :]
    live_last = live_tiles[:, :, None] - 1
    filled = jnp.where(slot_ids < live_last, TILE, jnp.where(slot_ids == live_last, last_fill[:, :, None], 0))
    return filled.astype(jnp.int32)


def draw_obs_tiles(key, part):
    draw_keys = jax.random.split(key, 2)
    lead_shape = (BLOCKS, BLOCKS, CAP)
    places = jax.random.uniform(draw_keys[0], lead_shape + (2, TILE), jnp.float32, 0.0, 1.0) * SB
    values = jax.random.normal(draw_keys[1], lead_shape + (FEAT - 2, TILE), jnp.float32)
    return jnp.concatenate([places, values], axis=3).astype(jnp.bfloat16)


def touch_ends(result, key, low, largest):
    index_at = [jax.random.randint(jax.random.fold_in(key, axis), (), 0, length) for axis, length in enumerate(result.shape)]
    longest = result.shape.index(max(result.shape))
    beside = index_at[:longest] + [(index_at[longest] + 1) % result.shape[longest]] + index_at[longest + 1:]
    return result.at[tuple(index_at)].set(low).at[tuple(beside)].set(largest)


def centred(own_key, dims, width, limit, held_as=jnp.bfloat16):
    entries = width * jax.random.normal(own_key, dims, jnp.float32)
    return jnp.clip(entries, min=-limit, max=limit).astype(held_as)


def setup_inputs(seed: int = 0) -> dict:
    arg_keys = jax.random.split(jax.random.key(seed), 9)
    obs_tiles = draw_obs_tiles(jax.random.fold_in(arg_keys[8], 71), 0)
    tile_block = touch_ends(jax.random.randint(arg_keys[1], (BLOCKS, BLOCKS, CAP), 0, SUBS), jax.random.fold_in(arg_keys[1], 1), 0, SUBS - 1).astype(jnp.int32)
    tile_rows = draw_tile_rows(jax.random.fold_in(arg_keys[8], 71), 0)
    embed_weight = centred(arg_keys[3], (FEAT - 2, CH0 - 1), (FEAT - 2) ** -0.5, 2.5)
    conv1_weight = centred(arg_keys[4], (9, CH0, C1), (9 * CH0) ** -0.5, 0.4375)
    conv1_bias = centred(arg_keys[5], (C1,), 0.5, 3.0, jnp.float32)
    conv2_weight = centred(arg_keys[6], (9, C1, C2), (9 * C1) ** -0.5, 0.125)
    conv2_bias = centred(arg_keys[7], (C2,), 0.5, 3.0, jnp.float32)
    return {"obs_tiles": obs_tiles, "tile_block": tile_block, "tile_rows": tile_rows, "embed_weight": embed_weight, "conv1_weight": conv1_weight, "conv1_bias": conv1_bias, "conv2_weight": conv2_weight, "conv2_bias": conv2_bias}


kernel_scale = 0.5


def tile_terms(tiles, row_count, embed_weight):
    cell_ids = jnp.arange(SB * SB, dtype=jnp.int32)
    center_row = (cell_ids // SB).astype(jnp.float32) + 0.5
    center_col = (cell_ids % SB).astype(jnp.float32) + 0.5
    place_row = tiles[:, 0, :].astype(jnp.float32)
    place_col = tiles[:, 1, :].astype(jnp.float32)
    distance = (center_row[None, :, None] - place_row[:, None, :]) ** 2 + (center_col[None, :, None] - place_col[:, None, :]) ** 2
    is_live = jnp.arange(tiles.shape[2], dtype=jnp.int32)[None, None, :] < row_count[:, None, None]
    kernel = jnp.where(is_live, jnp.exp(-distance * kernel_scale), jnp.float32(0.0)).astype(jnp.bfloat16)
    embedded = jnp.einsum('tvo,vc->tco', tiles[:, 2:, :].astype(jnp.float32), embed_weight.astype(jnp.float32)).astype(jnp.bfloat16)
    features = jnp.concatenate([jnp.ones((tiles.shape[0], 1, tiles.shape[2]), jnp.bfloat16), embedded], axis=1)
    return jnp.einsum('tco,tko->tck', features.astype(jnp.float32), kernel.astype(jnp.float32))


def stride_conv(padded, weight, out_rows, out_cols):
    running = jnp.zeros((out_rows * out_cols, weight.shape[2]), jnp.float32)
    for row_tap in range(3):
        for col_tap in range(3):
            tap_rows = lax.slice(padded, (row_tap, col_tap, 0), (row_tap + 2 * out_rows - 1, col_tap + 2 * out_cols - 1, padded.shape[2]), (2, 2, 1))
            running = running + jnp.dot(tap_rows.reshape(-1, padded.shape[2]), weight[3 * row_tap + col_tap], preferred_element_type=jnp.float32)
    return running.reshape(out_rows, out_cols, weight.shape[2])


def cycle_pad(field_in):
    wrapped = jnp.concatenate([field_in[:, -1:, :], field_in], axis=1)
    return jnp.concatenate([jnp.zeros((1,) + wrapped.shape[1:], field_in.dtype), wrapped], axis=0)


def reference(obs_tiles, tile_block, tile_rows, embed_weight, conv1_weight, conv1_bias, conv2_weight, conv2_bias):
    block_count = obs_tiles.shape[0]
    sub_count = (BX // SB) * (BY // SB)

    def one_source(running, inputs):
        tiles, block_ids, row_count = inputs
        tile_sums = tile_terms(tiles.reshape(-1, FEAT, TILE), row_count.reshape(-1), embed_weight)
        tile_sums = tile_sums.reshape(block_count, CAP, CH0, TILE)
        onehot = (block_ids[:, :, None] == jnp.arange(sub_count, dtype=jnp.int32)[None, None, :]).astype(jnp.float32)
        return running + jnp.einsum('dns,dnck->dsck', onehot, tile_sums, precision=lax.Precision.HIGHEST), None

    start = jnp.zeros((block_count, sub_count, CH0, TILE), jnp.float32)
    block_sums, _ = lax.scan(one_source, start, (obs_tiles, tile_block, tile_rows))
    density = block_sums[:, :, 0, :]
    data_part = block_sums[:, :, 1:, :] / (1.0 + density[:, :, None, :])
    channels = jnp.concatenate([jnp.log1p(density)[:, :, None, :], data_part], axis=2).astype(jnp.bfloat16)
    grid_field = channels.reshape(N_LAT, N_LON, BX // SB, BY // SB, CH0, SB, SB)
    grid_field = grid_field.transpose(0, 2, 5, 1, 3, 6, 4).reshape(NX, NY, CH0)
    first_layer = jax.nn.silu(stride_conv(cycle_pad(grid_field), conv1_weight, NX // 2, NY // 2) + conv1_bias).astype(jnp.bfloat16)
    coarse = (stride_conv(cycle_pad(first_layer), conv2_weight, NX // 4, NY // 4) + conv2_bias).astype(jnp.bfloat16)
    return coarse
```

```python
import jax
import jax.numpy as jnp
from jax import lax
from jax.experimental import pallas as pl
from jax.experimental.pallas import tpu as pltpu
from jax.sharding import PartitionSpec as P

BX = 64
BY = 48
SB = 16
TILE = 256
CAP = 4
FEAT = 8
C1 = 256
C2 = 512
SUBS = 12
PHASES = 4
QUADS = BY // PHASES
ROW_LANES = PHASES * FEAT
HALF_LANES = (BX // 2 + 4) * ROW_LANES
FAR = 8192.0
ROOT_HALF_LOG2E = (0.5 * 1.4426950408889634) ** 0.5
SOURCES = 16


def iota(shape, axis):
    return lax.broadcasted_iota(jnp.int32, shape, axis)


def setconv_kernel(sub_ref, core_ref, tiles_ref, mine_ref, send_ref, tail_ref, *sums):
    step = pl.program_id(0)

    @pl.when(step == 0)
    def _():
        for total in sums:
            total[...] = jnp.zeros_like(total)

    row = iota((SB, 1), 0)
    center_row = (row.astype(jnp.float32) + 0.5) * ROOT_HALF_LOG2E
    center_col = ((row % 4 * 4 + row // 4).astype(jnp.float32) + 0.5) * ROOT_HALF_LOG2E

    def add_tile(source, slot, total):
        tile = jnp.concatenate([tiles_ref[source, slot], tiles_ref[source, slot + CAP]], axis=1)
        place = tile.astype(jnp.float32)
        off_row = center_row - place[0:1] * ROOT_HALF_LOG2E
        off_col = center_col - place[1:2] * ROOT_HALF_LOG2E
        along_row = jnp.exp2(-(off_row * off_row)).astype(jnp.bfloat16)
        along_col = jnp.exp2(-(off_col * off_col)).astype(jnp.bfloat16)
        weighted = [along_row, jnp.zeros_like(along_row)]
        weighted += [tile[k : k + 1] * along_row for k in range(2, FEAT)]
        part = lax.dot_general(
            along_col,
            jnp.concatenate(weighted, axis=0),
            (((1,), (1,)), ((), ())),
            preferred_element_type=jnp.float32,
        )
        sub = sub_ref[step * SOURCES + source, slot]
        total[sub] = total[sub] + part

    def add_sources(m, carry):
        for k in range(4):
            for slot in range(CAP):
                add_tile(4 * m + k, slot, sums[slot])
        return carry

    lax.fori_loop(0, SOURCES // 4, add_sources, 0)

    @pl.when(step == pl.num_programs(0) - 1)
    def _():
        total = sums[0][...]
        for more in sums[1:]:
            total = total + more[...]
        total = total.reshape(SUBS * SB, FEAT * SB)
        pick = (iota((128, 128), 0) == iota((128, 128), 1) % SB).astype(jnp.float32)
        density = jnp.dot(
            total, pick, precision=lax.Precision.HIGHEST, preferred_element_type=jnp.float32
        )
        lane = iota((SUBS * SB, 128), 1)
        grid = jnp.where(lane < SB, jnp.log1p(density), total / (1.0 + density))
        grid = grid.astype(jnp.bfloat16)
        core = core_ref[0]
        target = iota((4 * 32, SUBS * SB), 0)
        source = iota((4 * 32, SUBS * SB), 1)
        quad = target % 32 - QUADS * core
        wanted = (target // 32) * BY + (quad // 4) * SB + quad % 4
        inside = (quad >= 0) & (quad < QUADS)
        parts = []
        for phase in range(PHASES):
            take = (inside & (source == wanted + 4 * phase)).astype(jnp.bfloat16)
            parts.append(
                jnp.dot(take, grid, preferred_element_type=jnp.float32).astype(jnp.bfloat16)
            )
        spread = jnp.concatenate(parts, axis=1)
        lane_in = iota((512, 512), 0)
        lane_out = iota((512, 512), 1)
        moved = (
            lane_in % SB * ROW_LANES + lane_in // 128 * FEAT + lane_in % 128 // SB == lane_out
        ).astype(jnp.bfloat16)
        ordered = jnp.dot(spread, moved, preferred_element_type=jnp.float32).astype(jnp.bfloat16)
        whole = jnp.concatenate(
            [ordered[32 * k : 32 * k + 2 * QUADS] for k in range(4)], axis=1
        )
        upper = jnp.concatenate([jnp.zeros((2 * QUADS, 128), jnp.bfloat16), whole[:, :1024]], axis=1)
        lower = whole[:, 896:]
        tail_ref[...] = whole[:, 1920:]

        @pl.when(core == 0)
        def _():
            mine_ref[...] = upper
            send_ref[...] = lower

        @pl.when(core != 0)
        def _():
            mine_ref[...] = lower
            send_ref[...] = upper


def set_convolution(subs, core, arrived):
    half = jax.ShapeDtypeStruct((2 * QUADS, HALF_LANES), jnp.bfloat16)
    tail = jax.ShapeDtypeStruct((2 * QUADS, 128), jnp.bfloat16)
    same = lambda i, *_: (0, 0)
    return pl.pallas_call(
        setconv_kernel,
        grid_spec=pltpu.PrefetchScalarGridSpec(
            num_scalar_prefetch=2,
            grid=(arrived.shape[0] // SOURCES,),
            in_specs=[pl.BlockSpec((SOURCES,) + arrived.shape[1:], lambda i, *_: (i, 0, 0, 0))],
            out_specs=[
                pl.BlockSpec(half.shape, same),
                pl.BlockSpec(half.shape, same),
                pl.BlockSpec(tail.shape, same),
            ],
            scratch_shapes=[pltpu.VMEM((SUBS, SB, FEAT * SB), jnp.float32)] * CAP,
        ),
        out_shape=[half, half, tail],
        compiler_params=pltpu.CompilerParams(
            dimension_semantics=("arbitrary",), vmem_limit_bytes=48 << 20
        ),
    )(subs, core, arrived)


def conv_kernel(
    top_ref, grid_ref, odd1_ref, odd2_ref, even1_ref, even2_ref, bias1_ref, weight2_ref,
    bias2_ref, out_ref, moved_ref, even_rows, odd_rows,
):
    step = pl.program_id(0)
    columns = grid_ref.shape[0]

    def first_row(t, step_rows):
        block = t // 2
        if t % 2 == 0:
            here = grid_ref[:, 128 * block : 128 * block + 128]
            left = moved_ref[:, 128 * block : 128 * block + 128]
            odd = jnp.dot(here, odd1_ref[...], preferred_element_type=jnp.float32)
            weights = even1_ref
        else:
            here = grid_ref[:, 128 * block : 128 * block + 256]
            left = moved_ref[:, 128 * block : 128 * block + 256]
            odd = jnp.dot(here, odd2_ref[...], preferred_element_type=jnp.float32)
            weights = even2_ref
        even = jnp.dot(
            jnp.concatenate([here, left], axis=1), weights[...], preferred_element_type=jnp.float32
        )

        def activate(half):
            half = half + bias1_ref[...]
            return half * jnp.tanh(half) + half

        odd = activate(odd)
        even = activate(even)
        if t == 0:
            live = top_ref[0].astype(jnp.float32)
            odd = odd * live
            even = even * live
        before = pltpu.roll(odd, 1, axis=0)
        store = even_rows if t % 2 == 0 else odd_rows
        at = pl.ds(block * columns, columns)
        store[at, 0:C1] = before.astype(jnp.bfloat16)
        store[at, C1 : 2 * C1] = even.astype(jnp.bfloat16)
        store[at, 2 * C1 :] = odd.astype(jnp.bfloat16)

    def second_rows(pair):
        total = None
        for tap, (store, at) in enumerate(
            [(even_rows, 2 * pair), (odd_rows, 2 * pair), (even_rows, 2 * pair + 1)]
        ):
            part = jnp.dot(
                store[at * columns : (at + 2) * columns, :],
                weight2_ref[tap],
                preferred_element_type=jnp.float32,
            )
            total = part if total is None else total + part
        total = (total + bias2_ref[...]).astype(jnp.bfloat16)
        out_ref[...] = total.reshape(out_ref.shape)

    @pl.when(step == 0)
    def _():
        moved_ref[...] = pltpu.roll(grid_ref[...].astype(jnp.float32), 1, axis=0).astype(
            jnp.bfloat16
        )
        first_row(0, 0)

    for pair in range(4):

        @pl.when(step == pair)
        def _(pair=pair):
            for t in range(4 * pair + 1, 4 * pair + 5):
                first_row(t, 0)
            second_rows(pair)


def convolutions(top, gathered, weights1, bias1, weights2, bias2):
    columns = gathered.shape[0]
    full = lambda a: pl.BlockSpec(a.shape, lambda i, *_: (0,) * a.ndim)
    operands = [gathered, *weights1, bias1, weights2, bias2]
    return pl.pallas_call(
        conv_kernel,
        grid_spec=pltpu.PrefetchScalarGridSpec(
            num_scalar_prefetch=1,
            grid=(4,),
            in_specs=[full(a) for a in operands],
            out_specs=pl.BlockSpec((2, columns, C2), lambda i, *_: (i, 0, 0)),
            scratch_shapes=[
                pltpu.VMEM(gathered.shape, jnp.bfloat16),
                pltpu.VMEM((9 * columns, 3 * C1), jnp.bfloat16),
                pltpu.VMEM((8 * columns, 3 * C1), jnp.bfloat16),
            ],
        ),
        out_shape=jax.ShapeDtypeStruct((8, columns, C2), jnp.bfloat16),
        compiler_params=pltpu.CompilerParams(
            dimension_semantics=("arbitrary",), vmem_limit_bytes=56 << 20
        ),
    )(top, *operands)


def first_weights(embed_weight, conv1_weight):
    channels = conv1_weight.astype(jnp.float32)
    values = jnp.einsum(
        "vc,tco->tvo",
        embed_weight.astype(jnp.float32),
        channels[:, 1:],
        precision=lax.Precision.HIGHEST,
    )
    taps = jnp.concatenate([channels[:, :1], jnp.zeros_like(channels[:, :1]), values], axis=1)
    taps = (0.5 * taps).astype(jnp.bfloat16).reshape(3, 3, FEAT, C1)

    def placed(part, above, below, phase):
        pads = ((above, below), (phase, PHASES - phase - part.shape[1]), (0, 0), (0, 0))
        return jnp.pad(part, pads).reshape(-1, C1)

    odd = [placed(taps, above, below, 1) for above, below in ((1, 0), (3, 2))]
    even = [
        jnp.concatenate(
            [placed(taps[:, 1:], above, below, 0), placed(taps[:, :1], above, below, 3)], axis=0
        )
        for above, below in ((1, 0), (3, 2))
    ]
    return odd + even


def shards(
    obs_tiles,
    tile_block,
    tile_rows,
    embed_weight,
    conv1_weight,
    conv1_bias,
    conv2_weight,
    conv2_bias,
):
    blocks = obs_tiles.shape[1]
    n_lon = lax.axis_size("lon")
    n_lat = lax.axis_size("lat")
    core = lax.axis_index("lon") % 2

    tiles = obs_tiles[0]
    dead = iota(tiles.shape, 3) >= tile_rows[0][:, :, None, None]
    tiles = jnp.where(dead & (iota(tiles.shape, 2) == 0), jnp.bfloat16(FAR), tiles)
    notes = jnp.pad(
        tile_block[0].astype(jnp.bfloat16)[:, None, None, :], ((0, 0), (0, 0), (0, 7), (0, 124))
    )
    leaving = jnp.concatenate([tiles[..., :128], tiles[..., 128:], notes], axis=1)
    arrived = lax.all_to_all(leaving, ("lat", "lon"), 0, 0, tiled=True)
    subs = arrived[:, 2 * CAP, 0, :CAP].astype(jnp.int32)
    mine, send, tail = set_convolution(subs, core.reshape(1), arrived)

    pairs = [(i, i ^ 1) for i in range(n_lon)]
    other = lax.ppermute(send, "lon", pairs)
    from_same = [
        (z * n_lon + i, (z + 1) * n_lon + i) for z in range(n_lat - 1) for i in range(0, n_lon, 2)
    ]
    from_other = [(a + 1, b) for a, b in from_same]
    halo = lax.ppermute(tail, ("lat", "lon"), from_same) + lax.ppermute(
        tail, ("lat", "lon"), from_other
    )
    joined = mine + other + jnp.pad(halo, ((0, 0), (0, HALF_LANES - 128)))
    groups = [[2 * k + c for k in range(n_lon // 2)] for c in range(2)]
    gathered = lax.all_gather(joined, "lon", axis=0, tiled=True, axis_index_groups=groups)

    weights1 = first_weights(embed_weight, conv1_weight)
    top = jnp.where((lax.axis_index("lat") == 0) & (core == 0), 0, 1).reshape(1)
    half = convolutions(
        top,
        gathered,
        weights1,
        0.5 * conv1_bias[None],
        conv2_weight.reshape(3, 3 * C1, C2),
        conv2_bias[None],
    )
    swapped = lax.ppermute(half, "lon", pairs)
    first = core == 0
    return jnp.concatenate(
        [jnp.where(first, half, swapped), jnp.where(first, swapped, half)], axis=0
    )


def solution(mesh):
    placed = (
        P(("lat", "lon"), None, None, None, None),
        P(("lat", "lon"), None, None),
        P(("lat", "lon"), None, None),
        P(),
        P(),
        P(),
        P(),
        P(),
    )
    return jax.shard_map(
        shards, mesh=mesh, in_specs=placed, out_specs=P("lat", None, None), check_vma=False
    )
```

```python
import jax
import jax.numpy as jnp
from jax import lax
from jax.experimental import pallas as pl
from jax.experimental.pallas import tpu as pltpu
from jax.sharding import PartitionSpec as P

BX = 64
BY = 48
SB = 16
TILE = 256
CAP = 4
FEAT = 8
C1 = 256
C2 = 512
SUBS = 12
PHASES = 4
QUADS = BY // PHASES
ROW_LANES = PHASES * FEAT
HALF_LANES = (BX // 2 + 4) * ROW_LANES
FAR = 8192.0
ROOT_HALF_LOG2E = (0.5 * 1.4426950408889634) ** 0.5
SOURCES = 16


def iota(shape, axis):
    return lax.broadcasted_iota(jnp.int32, shape, axis)


def setconv_kernel(sub_ref, core_ref, tiles_ref, mine_ref, send_ref, tail_ref, *sums):
    step = pl.program_id(0)

    @pl.when(step == 0)
    def _():
        for total in sums:
            total[...] = jnp.zeros_like(total)

    row = iota((SB, 1), 0)
    center_row = (row.astype(jnp.float32) + 0.5) * ROOT_HALF_LOG2E
    center_col = ((row % 4 * 4 + row // 4).astype(jnp.float32) + 0.5) * ROOT_HALF_LOG2E

    def add_tile(source, slot, total):
        tile = jnp.concatenate([tiles_ref[source, slot], tiles_ref[source, slot + CAP]], axis=1)
        place = tile.astype(jnp.float32)
        notes = tiles_ref[source, 2 * CAP]
        live = jnp.concatenate(
            [notes[2 * slot : 2 * slot + 1], notes[2 * slot + 1 : 2 * slot + 2]], axis=1
        )
        place_row = jnp.where(live.astype(jnp.float32) > 0.0, place[0:1], FAR)
        off_row = center_row - place_row * ROOT_HALF_LOG2E
        off_col = center_col - place[1:2] * ROOT_HALF_LOG2E
        along_row = jnp.exp2(-(off_row * off_row)).astype(jnp.bfloat16)
        along_col = jnp.exp2(-(off_col * off_col)).astype(jnp.bfloat16)
        weighted = [along_row, jnp.zeros_like(along_row)]
        weighted += [tile[k : k + 1] * along_row for k in range(2, FEAT)]
        part = lax.dot_general(
            along_col,
            jnp.concatenate(weighted, axis=0),
            (((1,), (1,)), ((), ())),
            preferred_element_type=jnp.float32,
        )
        sub = sub_ref[step * SOURCES + source, slot]
        total[sub] = total[sub] + part

    def add_sources(m, carry):
        for k in range(4):
            for slot in range(CAP):
                add_tile(4 * m + k, slot, sums[slot])
        return carry

    lax.fori_loop(0, SOURCES // 4, add_sources, 0)

    @pl.when(step == pl.num_programs(0) - 1)
    def _():
        total = sums[0][...]
        for more in sums[1:]:
            total = total + more[...]
        total = total.reshape(SUBS * SB, FEAT * SB)
        pick = (iota((128, 128), 0) == iota((128, 128), 1) % SB).astype(jnp.float32)
        density = jnp.dot(
            total, pick, precision=lax.Precision.HIGHEST, preferred_element_type=jnp.float32
        )
        lane = iota((SUBS * SB, 128), 1)
        grid = jnp.where(lane < SB, jnp.log1p(density), total / (1.0 + density))
        grid = grid.astype(jnp.bfloat16)
        core = core_ref[0]
        target = iota((4 * 32, SUBS * SB), 0)
        source = iota((4 * 32, SUBS * SB), 1)
        quad = target % 32 - QUADS * core
        wanted = (target // 32) * BY + (quad // 4) * SB + quad % 4
        inside = (quad >= 0) & (quad < QUADS)
        parts = []
        for phase in range(PHASES):
            take = (inside & (source == wanted + 4 * phase)).astype(jnp.bfloat16)
            parts.append(
                jnp.dot(take, grid, preferred_element_type=jnp.float32).astype(jnp.bfloat16)
            )
        spread = jnp.concatenate(parts, axis=1)
        lane_in = iota((512, 512), 0)
        lane_out = iota((512, 512), 1)
        moved = (
            lane_in % SB * ROW_LANES + lane_in // 128 * FEAT + lane_in % 128 // SB == lane_out
        ).astype(jnp.bfloat16)
        ordered = jnp.dot(spread, moved, preferred_element_type=jnp.float32).astype(jnp.bfloat16)
        whole = jnp.concatenate(
            [ordered[32 * k : 32 * k + 2 * QUADS] for k in range(4)], axis=1
        )
        upper = jnp.concatenate([jnp.zeros((2 * QUADS, 128), jnp.bfloat16), whole[:, :1024]], axis=1)
        lower = whole[:, 896:]
        tail_ref[...] = whole[:, 1920:]

        @pl.when(core == 0)
        def _():
            mine_ref[...] = upper
            send_ref[...] = lower

        @pl.when(core != 0)
        def _():
            mine_ref[...] = lower
            send_ref[...] = upper


def set_convolution(subs, core, arrived):
    half = jax.ShapeDtypeStruct((2 * QUADS, HALF_LANES), jnp.bfloat16)
    tail = jax.ShapeDtypeStruct((2 * QUADS, 128), jnp.bfloat16)
    same = lambda i, *_: (0, 0)
    return pl.pallas_call(
        setconv_kernel,
        grid_spec=pltpu.PrefetchScalarGridSpec(
            num_scalar_prefetch=2,
            grid=(arrived.shape[0] // SOURCES,),
            in_specs=[pl.BlockSpec((SOURCES,) + arrived.shape[1:], lambda i, *_: (i, 0, 0, 0))],
            out_specs=[
                pl.BlockSpec(half.shape, same),
                pl.BlockSpec(half.shape, same),
                pl.BlockSpec(tail.shape, same),
            ],
            scratch_shapes=[pltpu.VMEM((SUBS, SB, FEAT * SB), jnp.float32)] * CAP,
        ),
        out_shape=[half, half, tail],
        compiler_params=pltpu.CompilerParams(
            dimension_semantics=("arbitrary",), vmem_limit_bytes=48 << 20
        ),
    )(subs, core, arrived)


def conv_kernel(
    place_ref, near_ref, east1_ref, east2_ref, east3_ref, odd1_ref, odd2_ref, even1_ref, even2_ref,
    bias1_ref, weight2_ref, bias2_ref, *rest,
):
    out_ref, send_ref, grid_ref, moved_ref, even_rows, odd_rows = rest[-6:]
    step = pl.program_id(0)
    columns = grid_ref.shape[0]
    quarter = near_ref.shape[0]

    def first_row(t):
        block = t // 2
        if t % 2 == 0:
            here = grid_ref[:, 128 * block : 128 * block + 128]
            left = moved_ref[:, 128 * block : 128 * block + 128]
            odd = jnp.dot(here, odd1_ref[...], preferred_element_type=jnp.float32)
            weights = even1_ref
        else:
            here = grid_ref[:, 128 * block : 128 * block + 256]
            left = moved_ref[:, 128 * block : 128 * block + 256]
            odd = jnp.dot(here, odd2_ref[...], preferred_element_type=jnp.float32)
            weights = even2_ref
        even = jnp.dot(
            jnp.concatenate([here, left], axis=1), weights[...], preferred_element_type=jnp.float32
        )

        def activate(half):
            half = half + bias1_ref[...]
            return half * jnp.tanh(half) + half

        odd = activate(odd)
        even = activate(even)
        if t == 0:
            live = place_ref[2].astype(jnp.float32)
            odd = odd * live
            even = even * live
        before = pltpu.roll(odd, 1, axis=0)
        store = even_rows if t % 2 == 0 else odd_rows
        at = pl.ds(block * columns, columns)
        store[at, 0:C1] = before.astype(jnp.bfloat16)
        store[at, C1 : 2 * C1] = even.astype(jnp.bfloat16)
        store[at, 2 * C1 :] = odd.astype(jnp.bfloat16)

    def second_rows(pair):
        total = None
        for tap, (store, at) in enumerate(
            [(even_rows, 2 * pair), (odd_rows, 2 * pair), (even_rows, 2 * pair + 1)]
        ):
            part = jnp.dot(
                store[at * columns : (at + 2) * columns, :],
                weight2_ref[tap],
                preferred_element_type=jnp.float32,
            )
            total = part if total is None else total + part
        total = (total + bias2_ref[...]).astype(jnp.bfloat16).reshape(out_ref.shape)
        out_ref[...] = total
        send_ref[...] = total

    @pl.when(step == 0)
    def _():
        for k, piece in enumerate((near_ref, east1_ref, east2_ref, east3_ref)):
            at = pl.multiple_of((place_ref[1] + k) % 4 * quarter, quarter)
            grid_ref[pl.ds(at, quarter), :] = piece[...]
        moved_ref[...] = pltpu.roll(grid_ref[...].astype(jnp.float32), 1, axis=0).astype(
            jnp.bfloat16
        )
        for t in range(5):
            first_row(t)
        second_rows(0)

    @pl.when(step == 1)
    def _():
        for t in range(5, 9):
            first_row(t)
        second_rows(1)


def convolutions(part, place, pieces, weights1, bias1, weights2, bias2, whole):
    columns = 4 * pieces[0].shape[0]
    lanes = pieces[0].shape[1]
    full = lambda a: pl.BlockSpec(a.shape, lambda i, *_: (0,) * a.ndim)
    operands = [*pieces, *weights1, bias1, weights2, bias2]
    specs = [full(a) for a in operands]
    aliases = {}
    if whole is not None:
        aliases = {1 + len(operands): 0}
        operands.append(whole)
        specs.append(pl.BlockSpec(memory_space=pl.ANY))
    return pl.pallas_call(
        conv_kernel,
        grid_spec=pltpu.PrefetchScalarGridSpec(
            num_scalar_prefetch=1,
            grid=(2,),
            in_specs=specs,
            out_specs=[
                pl.BlockSpec((2, columns, C2), lambda i, place: (place[0] * 4 + 2 * part + i, 0, 0)),
                pl.BlockSpec((2, columns, C2), lambda i, *_: (i, 0, 0)),
            ],
            scratch_shapes=[
                pltpu.VMEM((columns, lanes), jnp.bfloat16),
                pltpu.VMEM((columns, lanes), jnp.bfloat16),
                pltpu.VMEM((5 * columns, 3 * C1), jnp.bfloat16),
                pltpu.VMEM((4 * columns, 3 * C1), jnp.bfloat16),
            ],
        ),
        out_shape=[
            jax.ShapeDtypeStruct((16, columns, C2), jnp.bfloat16),
            jax.ShapeDtypeStruct((4, columns, C2), jnp.bfloat16),
        ],
        input_output_aliases=aliases,
        compiler_params=pltpu.CompilerParams(
            dimension_semantics=("arbitrary",), vmem_limit_bytes=56 << 20
        ),
    )(place, *operands)


def first_weights(embed_weight, conv1_weight):
    channels = conv1_weight.astype(jnp.float32)
    values = jnp.einsum(
        "vc,tco->tvo",
        embed_weight.astype(jnp.float32),
        channels[:, 1:],
        precision=lax.Precision.HIGHEST,
    )
    taps = jnp.concatenate([channels[:, :1], jnp.zeros_like(channels[:, :1]), values], axis=1)
    taps = (0.5 * taps).astype(jnp.bfloat16).reshape(3, 3, FEAT, C1)

    def placed(part, above, below, phase):
        pads = ((above, below), (phase, PHASES - phase - part.shape[1]), (0, 0), (0, 0))
        return jnp.pad(part, pads).reshape(-1, C1)

    odd = [placed(taps, above, below, 1) for above, below in ((1, 0), (3, 2))]
    even = [
        jnp.concatenate(
            [placed(taps[:, 1:], above, below, 0), placed(taps[:, :1], above, below, 3)], axis=0
        )
        for above, below in ((1, 0), (3, 2))
    ]
    return odd + even


def shards(
    obs_tiles,
    tile_block,
    tile_rows,
    embed_weight,
    conv1_weight,
    conv1_bias,
    conv2_weight,
    conv2_bias,
):
    blocks = obs_tiles.shape[1]
    n_lon = lax.axis_size("lon")
    n_lat = lax.axis_size("lat")
    core = lax.axis_index("lon") % 2

    tiles = obs_tiles[0]
    lanes = iota((blocks, 2 * CAP, 128), 2) + 128 * (iota((blocks, 2 * CAP, 128), 1) % 2)
    twice = lambda a: jnp.repeat(a[0], 2, axis=1)[:, :, None]
    notes = jnp.where(lanes < twice(tile_rows), twice(tile_block) + 1, 0).astype(jnp.bfloat16)
    leaving = jnp.concatenate([tiles[..., :128], tiles[..., 128:], notes[:, None]], axis=1)
    arrived = lax.all_to_all(leaving, ("lat", "lon"), 0, 0, tiled=True)
    subs = jnp.maximum(arrived[:, 2 * CAP, ::2, 0].astype(jnp.int32) - 1, 0)
    mine, send, tail = set_convolution(subs, core.reshape(1), arrived)

    pairs = [(i, i ^ 1) for i in range(n_lon)]
    other = lax.ppermute(send, "lon", pairs)
    from_same = [
        (z * n_lon + i, (z + 1) * n_lon + i) for z in range(n_lat - 1) for i in range(0, n_lon, 2)
    ]
    from_other = [(a + 1, b) for a, b in from_same]
    halo = lax.ppermute(tail, ("lat", "lon"), from_same) + lax.ppermute(
        tail, ("lat", "lon"), from_other
    )
    joined = mine + other + jnp.pad(halo, ((0, 0), (0, HALF_LANES - 128)))
    weights1 = first_weights(embed_weight, conv1_weight)

    def ring(value, stride, size):
        def behind(i, k):
            at = i // stride % size
            return i + ((at - k) % size - at) * stride

        return [lax.ppermute(value, "lon", [(i, behind(i, k)) for i in range(n_lon)]) for k in (1, 2, 3)]

    lon = lax.axis_index("lon")
    at_x, at_y = lon // 8, lon // 2 % 4
    top = jnp.where((lax.axis_index("lat") == 0) & (core == 0), 0, 1)
    whole = None
    swapped = []
    for part in range(2):
        near = joined[:, 512 * part : 512 * part + 640]
        ys = [near] + ring(near, 2, 4)
        line = jnp.stack(ys + ys[:3])
        quarter = lax.dynamic_slice_in_dim(line, (4 - at_y) % 4, 4).reshape(-1, line.shape[2])
        pieces = [quarter] + ring(quarter, 8, 4)
        place = jnp.stack([core, at_x, top if part == 0 else jnp.ones_like(top)]).astype(jnp.int32)
        whole, half = convolutions(
            part,
            place,
            pieces,
            weights1,
            0.5 * conv1_bias[None],
            conv2_weight.reshape(3, 3 * C1, C2),
            conv2_bias[None],
            whole,
        )
        swapped.append(lax.ppermute(half, "lon", pairs))
    for part in range(2):
        whole = lax.dynamic_update_slice_in_dim(
            whole, swapped[part], (1 - core) * 8 + 4 * part, axis=0
        )
    return whole


def solution(mesh):
    placed = (
        P(("lat", "lon"), None, None, None, None),
        P(("lat", "lon"), None, None),
        P(("lat", "lon"), None, None),
        P(),
        P(),
        P(),
        P(),
        P(),
    )
    return jax.shard_map(
        shards, mesh=mesh, in_specs=placed, out_specs=P("lat", None, None), check_vma=False
    )
```

```python
import functools

import jax
import jax.numpy as jnp
from jax import lax
from jax.experimental import pallas as pl
from jax.experimental.pallas import tpu as pltpu
from jax.sharding import PartitionSpec as P

BX = 64
BY = 48
SB = 16
TILE = 256
CAP = 4
FEAT = 8
C1 = 256
C2 = 512
SUBS = 12
PHASES = 4
QUADS = BY // PHASES
ROW_LANES = PHASES * FEAT
FAR = 8192.0
ROOT_HALF_LOG2E = (0.5 * 1.4426950408889634) ** 0.5
SOURCES = 16


def iota(shape, axis):
    return lax.broadcasted_iota(jnp.int32, shape, axis)


def setconv_kernel(note_ref, tiles_ref, out_ref, *sums):
    step = pl.program_id(0)

    @pl.when(step == 0)
    def _():
        for total in sums:
            total[...] = jnp.zeros_like(total)

    row = iota((SB, 1), 0)
    lane = iota((1, TILE), 1)
    center_row = (row.astype(jnp.float32) + 0.5) * ROOT_HALF_LOG2E
    center_col = ((row % 4 * 4 + row // 4).astype(jnp.float32) + 0.5) * ROOT_HALF_LOG2E

    def add_tile(source, slot, total):
        tile = jnp.concatenate([tiles_ref[source, slot], tiles_ref[source, slot + CAP]], axis=1)
        place = tile.astype(jnp.float32)
        live = lane < note_ref[step * SOURCES + source, CAP + slot]
        place_row = jnp.where(live, place[0:1], FAR)
        off_row = center_row - place_row * ROOT_HALF_LOG2E
        off_col = center_col - place[1:2] * ROOT_HALF_LOG2E
        along_row = jnp.exp2(-(off_row * off_row)).astype(jnp.bfloat16)
        along_col = jnp.exp2(-(off_col * off_col)).astype(jnp.bfloat16)
        weighted = [along_row, jnp.zeros_like(along_row)]
        weighted += [tile[k : k + 1] * along_row for k in range(2, FEAT)]
        part = lax.dot_general(
            along_col,
            jnp.concatenate(weighted, axis=0),
            (((1,), (1,)), ((), ())),
            preferred_element_type=jnp.float32,
        )
        sub = note_ref[step * SOURCES + source, slot]
        total[sub] = total[sub] + part

    def add_sources(m, carry):
        for k in range(4):
            for slot in range(CAP):
                add_tile(4 * m + k, slot, sums[slot])
        return carry

    lax.fori_loop(0, SOURCES // 4, add_sources, 0)

    @pl.when(step == pl.num_programs(0) - 1)
    def _():
        total = sums[0][...]
        for more in sums[1:]:
            total = total + more[...]
        total = total.reshape(SUBS * SB, FEAT * SB)
        pick = (iota((128, 128), 0) == iota((128, 128), 1) % SB).astype(jnp.float32)
        density = jnp.dot(
            total, pick, precision=lax.Precision.HIGHEST, preferred_element_type=jnp.float32
        )
        lane = iota((SUBS * SB, 128), 1)
        grid = jnp.where(lane < SB, jnp.log1p(density), total / (1.0 + density))
        grid = grid.astype(jnp.bfloat16)
        target = iota((4 * SB, SUBS * SB), 0)
        source = iota((4 * SB, SUBS * SB), 1)
        quad = target % SB
        wanted = target // SB * BY + quad // 4 * SB + quad % 4
        parts = []
        for phase in range(PHASES):
            take = ((quad < QUADS) & (source == wanted + 4 * phase)).astype(jnp.bfloat16)
            parts.append(
                jnp.dot(take, grid, preferred_element_type=jnp.float32).astype(jnp.bfloat16)
            )
        spread = jnp.concatenate(parts, axis=1)
        lane_in = iota((512, 512), 0)
        lane_out = iota((512, 512), 1)
        moved = (
            lane_in % SB * ROW_LANES + lane_in // 128 * FEAT + lane_in % 128 // SB == lane_out
        ).astype(jnp.bfloat16)
        ordered = jnp.dot(spread, moved, preferred_element_type=jnp.float32).astype(jnp.bfloat16)
        to = iota((8 * QUADS, 4 * SB), 0)
        start = iota((8 * QUADS, 4 * SB), 1)
        for half in range(2):
            rows = None
            for k in range(4):
                take = (to // QUADS % 4 == k) & (
                    start == (2 * half + to // (4 * QUADS)) * SB + to % QUADS
                )
                part = jnp.dot(
                    take.astype(jnp.bfloat16),
                    ordered[:, 128 * k : 128 * k + 128],
                    preferred_element_type=jnp.float32,
                )
                rows = part if rows is None else rows + part
            rows = rows.astype(jnp.bfloat16)
            for k in range(out_ref.shape[0] // 2):
                out_ref[2 * k + half] = rows


def set_convolution(notes, arrived, copies):
    out = jax.ShapeDtypeStruct((copies, 8 * QUADS, 128), jnp.bfloat16)
    return pl.pallas_call(
        setconv_kernel,
        grid_spec=pltpu.PrefetchScalarGridSpec(
            num_scalar_prefetch=1,
            grid=(arrived.shape[0] // SOURCES,),
            in_specs=[pl.BlockSpec((SOURCES,) + arrived.shape[1:], lambda i, *_: (i, 0, 0, 0))],
            out_specs=pl.BlockSpec(out.shape, lambda i, *_: (0, 0, 0)),
            scratch_shapes=[pltpu.VMEM((SUBS, SB, FEAT * SB), jnp.float32)] * CAP,
        ),
        out_shape=out,
        compiler_params=pltpu.CompilerParams(
            dimension_semantics=("arbitrary",), vmem_limit_bytes=24 << 20
        ),
    )(notes, arrived)


def leave_kernel(tiles_ref, notes_ref, out_ref):
    out_ref[:, :CAP] = tiles_ref[:, :, :, :128]
    out_ref[:, CAP : 2 * CAP] = tiles_ref[:, :, :, 128:]
    out_ref[:, 2 * CAP] = notes_ref[...]


def leaving_tiles(tiles, notes):
    count = tiles.shape[0]
    return pl.pallas_call(
        leave_kernel,
        grid=(count // SOURCES,),
        in_specs=[
            pl.BlockSpec((SOURCES,) + tiles.shape[1:], lambda i: (i, 0, 0, 0)),
            pl.BlockSpec((SOURCES,) + notes.shape[1:], lambda i: (i, 0, 0)),
        ],
        out_specs=pl.BlockSpec((SOURCES, 2 * CAP + 1, FEAT, 128), lambda i: (i, 0, 0, 0)),
        out_shape=jax.ShapeDtypeStruct((count, 2 * CAP + 1, FEAT, 128), jnp.bfloat16),
        compiler_params=pltpu.CompilerParams(vmem_limit_bytes=60 << 20),
    )(tiles, notes)


def conv_kernel(first_block, *refs):
    (flag_ref, *halo, own_ref, odd1_ref, odd2_ref, even1_ref, even2_ref, bias1_ref, weight2_hbm,
     bias2_ref) = refs[: 9 + (first_block == 0)]
    out_ref, send_ref, wide_ref, grid_ref, moved_ref, even_rows, odd_rows, weight2_ref, sem = refs[-9:]
    step = pl.program_id(0)
    columns = grid_ref.shape[0]
    load = pltpu.make_async_copy(weight2_hbm, weight2_ref, sem)

    def first_row(t):
        block = t // 2
        if t % 2 == 0:
            here = grid_ref[:, 128 * block : 128 * block + 128]
            left = moved_ref[:, 128 * block : 128 * block + 128]
            odd = jnp.dot(here, odd1_ref[...], preferred_element_type=jnp.float32)
            weights = even1_ref
        else:
            here = grid_ref[:, 128 * block : 128 * block + 256]
            left = moved_ref[:, 128 * block : 128 * block + 256]
            odd = jnp.dot(here, odd2_ref[...], preferred_element_type=jnp.float32)
            weights = even2_ref
        even = jnp.dot(
            jnp.concatenate([here, left], axis=1), weights[...], preferred_element_type=jnp.float32
        )

        def activate(half):
            half = half + bias1_ref[...]
            return half * jnp.tanh(half) + half

        odd = activate(odd)
        even = activate(even)
        if t == 0:
            live = flag_ref[1].astype(jnp.float32)
            odd = odd * live
            even = even * live
        before = pltpu.roll(odd, 1, axis=0)
        store = even_rows if t % 2 == 0 else odd_rows
        at = pl.ds(block * columns, columns)
        store[at, 0:C1] = before.astype(jnp.bfloat16)
        store[at, C1 : 2 * C1] = even.astype(jnp.bfloat16)
        store[at, 2 * C1 :] = odd.astype(jnp.bfloat16)

    def second_rows(pair):
        total = None
        for tap, (store, at) in enumerate(
            [(even_rows, 2 * pair), (odd_rows, 2 * pair), (even_rows, 2 * pair + 1)]
        ):
            part = jnp.dot(
                store[at * columns : (at + 2) * columns, :],
                weight2_ref[tap],
                preferred_element_type=jnp.float32,
            )
            total = part if total is None else total + part
        total = (total + bias2_ref[...]).astype(jnp.bfloat16).reshape(out_ref.shape)
        out_ref[...] = total
        send_ref[...] = total

    @pl.when(step == 0)
    def _():
        load.start()
        for source in range(own_ref.shape[0]):
            own = own_ref[source].astype(jnp.float32)
            parts = [own[QUADS * k : QUADS * (k + 1)] for k in range(first_block, first_block + 4)]
            if first_block == 0:
                parts = [halo[0][source].astype(jnp.float32)[SB - QUADS :]] + parts
            else:
                parts = [own[QUADS * (first_block - 1) : QUADS * first_block]] + parts
            for k, part in enumerate(parts):
                wide_ref[QUADS * source : QUADS * (source + 1), 128 * k : 128 * (k + 1)] = part
        grid_ref[...] = wide_ref[...].astype(jnp.bfloat16)
        moved_ref[...] = pltpu.roll(wide_ref[...], 1, axis=0).astype(jnp.bfloat16)
        for t in range(5):
            first_row(t)
        load.wait()
        second_rows(0)

    @pl.when(step == 1)
    def _():
        for t in range(5, 9):
            first_row(t)
        second_rows(1)


def convolutions(part, flags, halo, own, weights1, bias1, weights2, bias2, whole):
    columns = QUADS * own.shape[0]
    full = lambda a: pl.BlockSpec(a.shape, lambda i, *_: (0,) * a.ndim)
    anywhere = pl.BlockSpec(memory_space=pl.ANY)
    operands = [own, *weights1, bias1, weights2, bias2]
    if part == 0:
        operands = [halo] + operands
    specs = [anywhere if a is weights2 else full(a) for a in operands]
    aliases = {}
    if whole is not None:
        aliases = {1 + len(operands): 0}
        operands.append(whole)
        specs.append(anywhere)
    return pl.pallas_call(
        functools.partial(conv_kernel, 4 * part),
        grid_spec=pltpu.PrefetchScalarGridSpec(
            num_scalar_prefetch=1,
            grid=(2,),
            in_specs=specs,
            out_specs=[
                pl.BlockSpec((2, columns, C2), lambda i, flags: (flags[0] * 4 + 2 * part + i, 0, 0)),
                pl.BlockSpec((2, columns, C2), lambda i, *_: (i, 0, 0)),
            ],
            scratch_shapes=[
                pltpu.VMEM((columns, 640), jnp.float32),
                pltpu.VMEM((columns, 640), jnp.bfloat16),
                pltpu.VMEM((columns, 640), jnp.bfloat16),
                pltpu.VMEM((5 * columns, 3 * C1), jnp.bfloat16),
                pltpu.VMEM((4 * columns, 3 * C1), jnp.bfloat16),
                pltpu.VMEM(weights2.shape, jnp.bfloat16),
                pltpu.SemaphoreType.DMA,
            ],
        ),
        out_shape=[
            jax.ShapeDtypeStruct((16, columns, C2), jnp.bfloat16),
            jax.ShapeDtypeStruct((4, columns, C2), jnp.bfloat16),
        ],
        input_output_aliases=aliases,
        cost_estimate=pl.CostEstimate(
            flops=9_000_000_000, transcendentals=1_800_000, bytes_accessed=12_000_000
        ),
        compiler_params=pltpu.CompilerParams(
            dimension_semantics=("arbitrary",), vmem_limit_bytes=61 << 20
        ),
    )(flags, *operands)


def first_weights(embed_weight, conv1_weight):
    channels = conv1_weight.astype(jnp.float32)
    values = jnp.einsum(
        "vc,tco->tvo",
        embed_weight.astype(jnp.float32),
        channels[:, 1:],
        precision=lax.Precision.HIGHEST,
    )
    taps = jnp.concatenate([channels[:, :1], jnp.zeros_like(channels[:, :1]), values], axis=1)
    taps = (0.5 * taps).astype(jnp.bfloat16).reshape(3, 3, FEAT, C1)

    def placed(part, above, below, phase):
        pads = ((above, below), (phase, PHASES - phase - part.shape[1]), (0, 0), (0, 0))
        return jnp.pad(part, pads).reshape(-1, C1)

    odd = [placed(taps, above, below, 1) for above, below in ((1, 0), (3, 2))]
    even = [
        jnp.concatenate(
            [placed(taps[:, 1:], above, below, 0), placed(taps[:, :1], above, below, 3)], axis=0
        )
        for above, below in ((1, 0), (3, 2))
    ]
    return odd + even


def shards(
    obs_tiles,
    tile_block,
    tile_rows,
    embed_weight,
    conv1_weight,
    conv1_bias,
    conv2_weight,
    conv2_bias,
):
    n_lon = lax.axis_size("lon")
    n_lat = lax.axis_size("lat")
    core = lax.axis_index("lon") % 2

    notes = jnp.concatenate([tile_block[0], tile_rows[0]], axis=1).astype(jnp.bfloat16)
    notes = jnp.pad(notes[:, None], ((0, 0), (0, 7), (0, 120)))
    arrived = lax.all_to_all(leaving_tiles(obs_tiles[0], notes), ("lat", "lon"), 0, 0, tiled=True)
    notes = arrived[:, 2 * CAP, 0, : 2 * CAP].astype(jnp.int32)

    own = lax.all_to_all(set_convolution(notes, arrived, n_lon), "lon", 0, 0, tiled=True)
    last = own[:, 8 * QUADS - SB :]
    south = [(z * n_lon + i, z * n_lon + i + 1) for z in range(n_lat) for i in range(0, n_lon, 2)]
    south += [(b, b + n_lon - 1) for _, b in south if b + n_lon < n_lat * n_lon]
    halo = lax.ppermute(last, ("lat", "lon"), south)

    weights1 = first_weights(embed_weight, conv1_weight)
    top = jnp.where((lax.axis_index("lat") == 0) & (core == 0), 0, 1)
    pairs = [(i, i ^ 1) for i in range(n_lon)]
    whole = None
    swapped = []
    for part in (1, 0):
        flags = jnp.stack([core, top if part == 0 else jnp.ones_like(top)]).astype(jnp.int32)
        whole, half = convolutions(
            part,
            flags,
            halo,
            own,
            weights1,
            0.5 * conv1_bias[None],
            conv2_weight.reshape(3, 3 * C1, C2),
            conv2_bias[None],
            whole,
        )
        swapped.append((part, lax.ppermute(half, "lon", pairs)))
    for part, rows in swapped:
        whole = lax.dynamic_update_slice_in_dim(whole, rows, (1 - core) * 8 + 4 * part, axis=0)
    return whole


def solution(mesh):
    placed = (
        P(("lat", "lon"), None, None, None, None),
        P(("lat", "lon"), None, None),
        P(("lat", "lon"), None, None),
        P(),
        P(),
        P(),
        P(),
        P(),
    )
    return jax.shard_map(
        shards, mesh=mesh, in_specs=placed, out_specs=P("lat", None, None), check_vma=False
    )
```

```python
import functools

import jax
import jax.numpy as jnp
from jax import lax
from jax.experimental import pallas as pl
from jax.experimental.pallas import tpu as pltpu
from jax.sharding import PartitionSpec as P

BX = 64
BY = 48
SB = 16
TILE = 256
CAP = 4
FEAT = 8
KEPT = 7
C1 = 256
C2 = 512
SUBS = 12
PHASES = 4
QUADS = BY // PHASES
ROW_LANES = PHASES * FEAT
FAR = 8192.0
ROOT_HALF_LOG2E = (0.5 * 1.4426950408889634) ** 0.5
SOURCES = 16


def iota(shape, axis):
    return lax.broadcasted_iota(jnp.int32, shape, axis)


def setconv_kernel(note_ref, tiles_ref, out_ref, *sums):
    step = pl.program_id(0)

    @pl.when(step == 0)
    def _():
        for total in sums:
            total[...] = jnp.zeros_like(total)

    row = iota((SB, 1), 0)
    lane = iota((1, TILE), 1)
    center_row = (row.astype(jnp.float32) + 0.5) * ROOT_HALF_LOG2E
    center_col = ((row % 4 * 4 + row // 4).astype(jnp.float32) + 0.5) * ROOT_HALF_LOG2E

    def add_tile(source, slot, total):
        tile = jnp.concatenate([tiles_ref[source, slot], tiles_ref[source, slot + CAP]], axis=1)
        place = tile.astype(jnp.float32)
        live = lane < note_ref[step * SOURCES + source, CAP + slot]
        place_row = jnp.where(live, place[0:1], FAR)
        off_row = center_row - place_row * ROOT_HALF_LOG2E
        off_col = center_col - place[1:2] * ROOT_HALF_LOG2E
        along_row = jnp.exp2(-(off_row * off_row)).astype(jnp.bfloat16)
        along_col = jnp.exp2(-(off_col * off_col)).astype(jnp.bfloat16)
        weighted = [along_row]
        weighted += [tile[k : k + 1] * along_row for k in range(2, FEAT)]
        part = lax.dot_general(
            along_col,
            jnp.concatenate(weighted, axis=0),
            (((1,), (1,)), ((), ())),
            preferred_element_type=jnp.float32,
        )
        sub = note_ref[step * SOURCES + source, slot]
        total[sub] = total[sub] + part

    for k in range(SOURCES):
        for slot in range(CAP):
            add_tile(k, slot, sums[slot])

    @pl.when(step == pl.num_programs(0) - 1)
    def _():
        total = sums[0][...]
        for more in sums[1:]:
            total = total + more[...]
        total = total.reshape(SUBS * SB, KEPT * SB)
        total = jnp.concatenate([total, jnp.zeros((SUBS * SB, SB), jnp.float32)], axis=1)
        pick = (iota((128, 128), 0) == iota((128, 128), 1) % SB).astype(jnp.float32)
        density = jnp.dot(
            total, pick, precision=lax.Precision.HIGHEST, preferred_element_type=jnp.float32
        )
        lane = iota((SUBS * SB, 128), 1)
        grid = jnp.where(lane < SB, jnp.log1p(density), total / (1.0 + density))
        grid = grid.astype(jnp.bfloat16)
        target = iota((4 * SB, SUBS * SB), 0)
        source = iota((4 * SB, SUBS * SB), 1)
        quad = target % SB
        wanted = target // SB * BY + quad // 4 * SB + quad % 4
        parts = []
        for phase in range(PHASES):
            take = ((quad < QUADS) & (source == wanted + 4 * phase)).astype(jnp.bfloat16)
            parts.append(
                jnp.dot(take, grid, preferred_element_type=jnp.float32).astype(jnp.bfloat16)
            )
        spread = jnp.concatenate(parts, axis=1)
        lane_in = iota((512, 512), 0)
        lane_out = iota((512, 512), 1)
        moved = (
            lane_in % SB * ROW_LANES + lane_in // 128 * FEAT + lane_in % 128 // SB == lane_out
        ).astype(jnp.bfloat16)
        ordered = jnp.dot(spread, moved, preferred_element_type=jnp.float32).astype(jnp.bfloat16)
        to = iota((8 * QUADS, 4 * SB), 0)
        start = iota((8 * QUADS, 4 * SB), 1)
        for half in range(2):
            rows = None
            for k in range(4):
                take = (to // QUADS % 4 == k) & (
                    start == (2 * half + to // (4 * QUADS)) * SB + to % QUADS
                )
                part = jnp.dot(
                    take.astype(jnp.bfloat16),
                    ordered[:, 128 * k : 128 * k + 128],
                    preferred_element_type=jnp.float32,
                )
                rows = part if rows is None else rows + part
            rows = rows.astype(jnp.bfloat16)
            for k in range(out_ref.shape[0] // 2):
                out_ref[2 * k + half] = rows


def set_convolution(notes, arrived, copies):
    out = jax.ShapeDtypeStruct((copies, 8 * QUADS, 128), jnp.bfloat16)
    return pl.pallas_call(
        setconv_kernel,
        grid_spec=pltpu.PrefetchScalarGridSpec(
            num_scalar_prefetch=1,
            grid=(arrived.shape[0] // SOURCES,),
            in_specs=[pl.BlockSpec((SOURCES,) + arrived.shape[1:], lambda i, *_: (i, 0, 0, 0))],
            out_specs=pl.BlockSpec(out.shape, lambda i, *_: (0, 0, 0)),
            scratch_shapes=[pltpu.VMEM((SUBS, SB, KEPT * SB), jnp.float32)] * CAP,
        ),
        out_shape=out,
        compiler_params=pltpu.CompilerParams(
            dimension_semantics=("arbitrary",), vmem_limit_bytes=24 << 20
        ),
    )(notes, arrived)


def leave_kernel(sub_ref, rows_ref, tiles_ref, out_ref, notes_ref):
    step = pl.program_id(0)
    count = tiles_ref.shape[0]

    @pl.when(step == 0)
    def _():
        both = jnp.concatenate([sub_ref[...], rows_ref[...]], axis=0).astype(jnp.float32)
        blank = jnp.zeros((128 - 2 * CAP, both.shape[1]), jnp.float32)
        notes_ref[...] = jnp.concatenate([both, blank], axis=0).T

    notes = notes_ref[pl.ds(step * count, count), :]
    notes = jnp.broadcast_to(notes[:, None, :], (count, FEAT, 128)).astype(jnp.bfloat16)
    out_ref[:, :CAP] = tiles_ref[:, :, :, :128]
    out_ref[:, CAP : 2 * CAP] = tiles_ref[:, :, :, 128:]
    out_ref[:, 2 * CAP] = notes


def leaving_tiles(tiles, subs, rows):
    count = tiles.shape[0]
    part = count // 2
    return pl.pallas_call(
        leave_kernel,
        grid=(2,),
        in_specs=[
            pl.BlockSpec(subs.shape, lambda i: (0, 0)),
            pl.BlockSpec(rows.shape, lambda i: (0, 0)),
            pl.BlockSpec((part,) + tiles.shape[1:], lambda i: (i, 0, 0, 0)),
        ],
        out_specs=pl.BlockSpec((part, 2 * CAP + 1, FEAT, 128), lambda i: (i, 0, 0, 0)),
        out_shape=jax.ShapeDtypeStruct((count, 2 * CAP + 1, FEAT, 128), jnp.bfloat16),
        scratch_shapes=[pltpu.VMEM((count, 128), jnp.float32)],
        compiler_params=pltpu.CompilerParams(vmem_limit_bytes=60 << 20),
    )(subs, rows, tiles)


def conv_kernel(first_block, *refs):
    (flag_ref, *halo, own_ref, odd1_ref, odd2_ref, even1_ref, even2_ref, bias1_ref, weight2_hbm,
     bias2_ref) = refs[: 9 + (first_block == 0)]
    out_ref, send_ref, wide_ref, grid_ref, moved_ref, even_rows, odd_rows, weight2_ref, sem = refs[-9:]
    step = pl.program_id(0)
    columns = grid_ref.shape[0]
    loads = [
        pltpu.make_async_copy(
            weight2_hbm.at[tap, pl.ds(C1 * k, C1)], weight2_ref.at[tap, pl.ds(C1 * k, C1)], sem.at[tap, k]
        )
        for tap in range(3)
        for k in range(3)
    ]

    def first_row(t):
        block = t // 2
        if t % 2 == 0:
            here = grid_ref[:, 128 * block : 128 * block + 128]
            left = moved_ref[:, 128 * block : 128 * block + 128]
            odd = jnp.dot(here, odd1_ref[...], preferred_element_type=jnp.float32)
            weights = even1_ref
        else:
            here = grid_ref[:, 128 * block : 128 * block + 256]
            left = moved_ref[:, 128 * block : 128 * block + 256]
            odd = jnp.dot(here, odd2_ref[...], preferred_element_type=jnp.float32)
            weights = even2_ref
        even = jnp.dot(
            jnp.concatenate([here, left], axis=1), weights[...], preferred_element_type=jnp.float32
        )

        def activate(half):
            half = half + bias1_ref[...]
            return half * jnp.tanh(half) + half

        odd = activate(odd)
        even = activate(even)
        if t == 0:
            live = flag_ref[1].astype(jnp.float32)
            odd = odd * live
            even = even * live
        before = pltpu.roll(odd, 1, axis=0)
        store = even_rows if t % 2 == 0 else odd_rows
        at = pl.ds(block * columns, columns)
        store[at, 0:C1] = before.astype(jnp.bfloat16)
        store[at, C1 : 2 * C1] = even.astype(jnp.bfloat16)
        store[at, 2 * C1 :] = odd.astype(jnp.bfloat16)

    def second_row(row):
        total = None
        for tap, (store, at) in enumerate(
            [(even_rows, row), (odd_rows, row), (even_rows, row + 1)]
        ):
            part = jnp.dot(
                store[at * columns : (at + 1) * columns, :],
                weight2_ref[tap],
                preferred_element_type=jnp.float32,
            )
            total = part if total is None else total + part
        total = (total + bias2_ref[...]).astype(jnp.bfloat16).reshape(out_ref.shape)
        out_ref[...] = total
        send_ref[...] = total

    @pl.when(step == 0)
    def _():
        for load in loads:
            load.start()
        for source in range(own_ref.shape[0]):
            own = own_ref[source].astype(jnp.float32)
            parts = [own[QUADS * k : QUADS * (k + 1)] for k in range(first_block, first_block + 4)]
            if first_block == 0:
                parts = [halo[0][source].astype(jnp.float32)[SB - QUADS :]] + parts
            else:
                parts = [own[QUADS * (first_block - 1) : QUADS * first_block]] + parts
            for k, part in enumerate(parts):
                wide_ref[QUADS * source : QUADS * (source + 1), 128 * k : 128 * (k + 1)] = part
        grid_ref[...] = wide_ref[...].astype(jnp.bfloat16)
        moved_ref[...] = pltpu.roll(wide_ref[...], 1, axis=0).astype(jnp.bfloat16)
        for t in range(3):
            first_row(t)
        for load in loads:
            load.wait()
        second_row(0)

    for row in range(1, 4):

        @pl.when(step == row)
        def _(row=row):
            first_row(2 * row + 1)
            first_row(2 * row + 2)
            second_row(row)


def convolutions(part, flags, halo, own, weights1, bias1, weights2, bias2, whole):
    columns = QUADS * own.shape[0]
    full = lambda a: pl.BlockSpec(a.shape, lambda i, *_: (0,) * a.ndim)
    anywhere = pl.BlockSpec(memory_space=pl.ANY)
    operands = [own, *weights1, bias1, weights2, bias2]
    if part == 0:
        operands = [halo] + operands
    specs = [anywhere if a is weights2 else full(a) for a in operands]
    aliases = {}
    if whole is not None:
        aliases = {1 + len(operands): 0}
        operands.append(whole)
        specs.append(anywhere)
    return pl.pallas_call(
        functools.partial(conv_kernel, 4 * part),
        grid_spec=pltpu.PrefetchScalarGridSpec(
            num_scalar_prefetch=1,
            grid=(4,),
            in_specs=specs,
            out_specs=[
                pl.BlockSpec((1, columns, C2), lambda i, flags: (flags[0] * 8 + 4 * part + i, 0, 0)),
                pl.BlockSpec((1, columns, C2), lambda i, *_: (i, 0, 0)),
            ],
            scratch_shapes=[
                pltpu.VMEM((columns, 640), jnp.float32),
                pltpu.VMEM((columns, 640), jnp.bfloat16),
                pltpu.VMEM((columns, 640), jnp.bfloat16),
                pltpu.VMEM((5 * columns, 3 * C1), jnp.bfloat16),
                pltpu.VMEM((4 * columns, 3 * C1), jnp.bfloat16),
                pltpu.VMEM(weights2.shape, jnp.bfloat16),
                pltpu.SemaphoreType.DMA((3, 3)),
            ],
        ),
        out_shape=[
            jax.ShapeDtypeStruct((16, columns, C2), jnp.bfloat16),
            jax.ShapeDtypeStruct((4, columns, C2), jnp.bfloat16),
        ],
        input_output_aliases=aliases,
        cost_estimate=pl.CostEstimate(
            flops=9_000_000_000, transcendentals=1_800_000, bytes_accessed=12_000_000
        ),
        compiler_params=pltpu.CompilerParams(
            dimension_semantics=("arbitrary",), vmem_limit_bytes=40 << 20
        ),
    )(flags, *operands)


def first_weights(embed_weight, conv1_weight):
    channels = conv1_weight.astype(jnp.float32)
    values = jnp.einsum(
        "vc,tco->tvo",
        embed_weight.astype(jnp.float32),
        channels[:, 1:],
        precision=lax.Precision.HIGHEST,
    )
    taps = jnp.concatenate([channels[:, :1], values, jnp.zeros_like(channels[:, :1])], axis=1)
    taps = (0.5 * taps).astype(jnp.bfloat16).reshape(3, 3, FEAT, C1)

    def placed(part, above, below, phase):
        pads = ((above, below), (phase, PHASES - phase - part.shape[1]), (0, 0), (0, 0))
        return jnp.pad(part, pads).reshape(-1, C1)

    odd = [placed(taps, above, below, 1) for above, below in ((1, 0), (3, 2))]
    even = [
        jnp.concatenate(
            [placed(taps[:, 1:], above, below, 0), placed(taps[:, :1], above, below, 3)], axis=0
        )
        for above, below in ((1, 0), (3, 2))
    ]
    return odd + even


def shards(
    obs_tiles,
    tile_block,
    tile_rows,
    embed_weight,
    conv1_weight,
    conv1_bias,
    conv2_weight,
    conv2_bias,
):
    n_lon = lax.axis_size("lon")
    n_lat = lax.axis_size("lat")
    core = lax.axis_index("lon") % 2

    leaving = leaving_tiles(obs_tiles[0], tile_block[0].T, tile_rows[0].T)
    arrived = lax.all_to_all(leaving, ("lat", "lon"), 0, 0, tiled=True)
    notes = arrived[:, 2 * CAP, 0, : 2 * CAP].astype(jnp.int32)

    own = lax.all_to_all(set_convolution(notes, arrived, n_lon), "lon", 0, 0, tiled=True)
    last = own[:, 8 * QUADS - SB :]
    south = [(z * n_lon + i, z * n_lon + i + 1) for z in range(n_lat) for i in range(0, n_lon, 2)]
    south += [(b, b + n_lon - 1) for _, b in south if b + n_lon < n_lat * n_lon]
    halo = lax.ppermute(last, ("lat", "lon"), south)

    weights1 = first_weights(embed_weight, conv1_weight)
    top = jnp.where((lax.axis_index("lat") == 0) & (core == 0), 0, 1)
    pairs = [(i, i ^ 1) for i in range(n_lon)]
    whole = None
    swapped = []
    for part in (1, 0):
        flags = jnp.stack([core, top if part == 0 else jnp.ones_like(top)]).astype(jnp.int32)
        whole, half = convolutions(
            part,
            flags,
            halo,
            own,
            weights1,
            0.5 * conv1_bias[None],
            conv2_weight.reshape(3, 3 * C1, C2),
            conv2_bias[None],
            whole,
        )
        swapped.append((part, lax.ppermute(half, "lon", pairs)))
    for part, rows in swapped:
        whole = lax.dynamic_update_slice_in_dim(whole, rows, (1 - core) * 8 + 4 * part, axis=0)
    return whole


def solution(mesh):
    placed = (
        P(("lat", "lon"), None, None, None, None),
        P(("lat", "lon"), None, None),
        P(("lat", "lon"), None, None),
        P(),
        P(),
        P(),
        P(),
        P(),
    )
    return jax.shard_map(
        shards, mesh=mesh, in_specs=placed, out_specs=P("lat", None, None), check_vma=False
    )
```

```python
import functools

import jax
import jax.numpy as jnp
from jax import lax
from jax.experimental import pallas as pl
from jax.experimental.pallas import tpu as pltpu
from jax.sharding import PartitionSpec as P

BX = 64
BY = 48
SB = 16
TILE = 256
CAP = 4
FEAT = 8
KEPT = 7
C1 = 256
C2 = 512
SUBS = 12
PHASES = 4
QUADS = BY // PHASES
ROW_LANES = PHASES * FEAT
FAR = 8192.0
ROOT_HALF_LOG2E = (0.5 * 1.4426950408889634) ** 0.5
SOURCES = 32


def iota(shape, axis):
    return lax.broadcasted_iota(jnp.int32, shape, axis)


def setconv_kernel(note_ref, tiles_ref, out_ref, *sums):
    step = pl.program_id(0)

    @pl.when(step == 0)
    def _():
        for total in sums:
            total[...] = jnp.zeros_like(total)

    row = iota((SB, 1), 0)
    lane = iota((1, TILE), 1)
    center_row = (row.astype(jnp.float32) + 0.5) * ROOT_HALF_LOG2E
    center_col = ((row % 4 * 4 + row // 4).astype(jnp.float32) + 0.5) * ROOT_HALF_LOG2E

    def add_tile(source, slot, total):
        tile = jnp.concatenate([tiles_ref[source, slot], tiles_ref[source, slot + CAP]], axis=1)
        place = tile.astype(jnp.float32)
        live = lane < note_ref[step * SOURCES + source, CAP + slot]
        place_row = jnp.where(live, place[0:1], FAR)
        off_row = center_row - place_row * ROOT_HALF_LOG2E
        off_col = center_col - place[1:2] * ROOT_HALF_LOG2E
        along_row = jnp.exp2(-(off_row * off_row)).astype(jnp.bfloat16)
        along_col = jnp.exp2(-(off_col * off_col)).astype(jnp.bfloat16)
        weighted = [along_row]
        weighted += [tile[k : k + 1] * along_row for k in range(2, FEAT)]
        part = lax.dot_general(
            along_col,
            jnp.concatenate(weighted, axis=0),
            (((1,), (1,)), ((), ())),
            preferred_element_type=jnp.float32,
        )
        sub = note_ref[step * SOURCES + source, slot]
        total[sub] = total[sub] + part

    for k in range(SOURCES):
        for slot in range(CAP):
            add_tile(k, slot, sums[slot])

    @pl.when(step == pl.num_programs(0) - 1)
    def _():
        total = sums[0][...]
        for more in sums[1:]:
            total = total + more[...]
        total = total.reshape(SUBS * SB, KEPT * SB)
        total = jnp.concatenate([total, jnp.zeros((SUBS * SB, SB), jnp.float32)], axis=1)
        pick = (iota((128, 128), 0) == iota((128, 128), 1) % SB).astype(jnp.float32)
        density = jnp.dot(
            total, pick, precision=lax.Precision.HIGHEST, preferred_element_type=jnp.float32
        )
        lane = iota((SUBS * SB, 128), 1)
        grid = jnp.where(lane < SB, jnp.log1p(density), total / (1.0 + density))
        grid = grid.astype(jnp.bfloat16)
        target = iota((4 * SB, SUBS * SB), 0)
        source = iota((4 * SB, SUBS * SB), 1)
        quad = target % SB
        wanted = target // SB * BY + quad // 4 * SB + quad % 4
        parts = []
        for phase in range(PHASES):
            take = ((quad < QUADS) & (source == wanted + 4 * phase)).astype(jnp.bfloat16)
            parts.append(
                jnp.dot(take, grid, preferred_element_type=jnp.float32).astype(jnp.bfloat16)
            )
        spread = jnp.concatenate(parts, axis=1)
        lane_in = iota((512, 512), 0)
        lane_out = iota((512, 512), 1)
        moved = (
            lane_in % SB * ROW_LANES + lane_in // 128 * FEAT + lane_in % 128 // SB == lane_out
        ).astype(jnp.bfloat16)
        ordered = jnp.dot(spread, moved, preferred_element_type=jnp.float32).astype(jnp.bfloat16)
        to = iota((8 * QUADS, 4 * SB), 0)
        start = iota((8 * QUADS, 4 * SB), 1)
        for half in range(2):
            rows = None
            for k in range(4):
                take = (to // QUADS % 4 == k) & (
                    start == (2 * half + to // (4 * QUADS)) * SB + to % QUADS
                )
                part = jnp.dot(
                    take.astype(jnp.bfloat16),
                    ordered[:, 128 * k : 128 * k + 128],
                    preferred_element_type=jnp.float32,
                )
                rows = part if rows is None else rows + part
            rows = rows.astype(jnp.bfloat16)
            for k in range(out_ref.shape[0] // 2):
                out_ref[2 * k + half] = rows


def set_convolution(notes, arrived, copies):
    out = jax.ShapeDtypeStruct((copies, 8 * QUADS, 128), jnp.bfloat16)
    return pl.pallas_call(
        setconv_kernel,
        grid_spec=pltpu.PrefetchScalarGridSpec(
            num_scalar_prefetch=1,
            grid=(arrived.shape[0] // SOURCES,),
            in_specs=[pl.BlockSpec((SOURCES,) + arrived.shape[1:], lambda i, *_: (i, 0, 0, 0))],
            out_specs=pl.BlockSpec(out.shape, lambda i, *_: (0, 0, 0)),
            scratch_shapes=[pltpu.VMEM((SUBS, SB, KEPT * SB), jnp.float32)] * CAP,
        ),
        out_shape=out,
        compiler_params=pltpu.CompilerParams(
            dimension_semantics=("arbitrary",), vmem_limit_bytes=24 << 20
        ),
    )(notes, arrived)


def leave_kernel(sub_ref, rows_ref, tiles_ref, out_ref, notes_ref):
    step = pl.program_id(0)
    count = tiles_ref.shape[0]

    @pl.when(step == 0)
    def _():
        both = jnp.concatenate([sub_ref[...], rows_ref[...]], axis=0).astype(jnp.float32)
        blank = jnp.zeros((128 - 2 * CAP, both.shape[1]), jnp.float32)
        notes_ref[...] = jnp.concatenate([both, blank], axis=0).T

    notes = notes_ref[pl.ds(step * count, count), :]
    notes = jnp.broadcast_to(notes[:, None, :], (count, FEAT, 128)).astype(jnp.bfloat16)
    out_ref[:, :CAP] = tiles_ref[:, :, :, :128]
    out_ref[:, CAP : 2 * CAP] = tiles_ref[:, :, :, 128:]
    out_ref[:, 2 * CAP] = notes


def leaving_tiles(tiles, subs, rows):
    count = tiles.shape[0]
    part = count // 2
    return pl.pallas_call(
        leave_kernel,
        grid=(2,),
        in_specs=[
            pl.BlockSpec(subs.shape, lambda i: (0, 0)),
            pl.BlockSpec(rows.shape, lambda i: (0, 0)),
            pl.BlockSpec((part,) + tiles.shape[1:], lambda i: (i, 0, 0, 0)),
        ],
        out_specs=pl.BlockSpec((part, 2 * CAP + 1, FEAT, 128), lambda i: (i, 0, 0, 0)),
        out_shape=jax.ShapeDtypeStruct((count, 2 * CAP + 1, FEAT, 128), jnp.bfloat16),
        scratch_shapes=[pltpu.VMEM((count, 128), jnp.float32)],
        compiler_params=pltpu.CompilerParams(vmem_limit_bytes=60 << 20),
    )(subs, rows, tiles)


def conv_kernel(first_block, *refs):
    (flag_ref, *halo, own_ref, odd1_ref, odd2_ref, even1_ref, even2_ref, bias1_ref, weight2_hbm,
     bias2_ref) = refs[: 9 + (first_block == 0)]
    out_ref, send_ref, wide_ref, grid_ref, moved_ref, even_rows, odd_rows, weight2_ref, sem = refs[-9:]
    step = pl.program_id(0)
    columns = grid_ref.shape[0]
    loads = [
        pltpu.make_async_copy(
            weight2_hbm.at[tap, pl.ds(C1 * k, C1)], weight2_ref.at[tap, pl.ds(C1 * k, C1)], sem.at[tap, k]
        )
        for tap in range(3)
        for k in range(3)
    ]

    def first_row(t):
        block = t // 2
        if t % 2 == 0:
            here = grid_ref[:, 128 * block : 128 * block + 128]
            left = moved_ref[:, 128 * block : 128 * block + 128]
            odd = jnp.dot(here, odd1_ref[...], preferred_element_type=jnp.float32)
            weights = even1_ref
        else:
            here = grid_ref[:, 128 * block : 128 * block + 256]
            left = moved_ref[:, 128 * block : 128 * block + 256]
            odd = jnp.dot(here, odd2_ref[...], preferred_element_type=jnp.float32)
            weights = even2_ref
        even = jnp.dot(
            jnp.concatenate([here, left], axis=1), weights[...], preferred_element_type=jnp.float32
        )

        def activate(half):
            half = half + bias1_ref[...]
            return half * jnp.tanh(half) + half

        odd = activate(odd)
        even = activate(even)
        if t == 0:
            live = flag_ref[1].astype(jnp.float32)
            odd = odd * live
            even = even * live
        before = pltpu.roll(odd, 1, axis=0)
        store = even_rows if t % 2 == 0 else odd_rows
        at = pl.ds(block * columns, columns)
        store[at, 0:C1] = odd.astype(jnp.bfloat16)
        store[at, C1 : 2 * C1] = even.astype(jnp.bfloat16)
        store[at, 2 * C1 :] = before.astype(jnp.bfloat16)

    def second_row(row):
        total = None
        for tap, (store, at) in enumerate(
            [(even_rows, row), (odd_rows, row), (even_rows, row + 1)]
        ):
            part = jnp.dot(
                store[at * columns : (at + 1) * columns, :],
                weight2_ref[tap],
                preferred_element_type=jnp.float32,
            )
            total = part if total is None else total + part
        total = (total + bias2_ref[...]).astype(jnp.bfloat16).reshape(out_ref.shape)
        out_ref[...] = total
        send_ref[...] = total

    @pl.when(step == 0)
    def _():
        for load in loads:
            load.start()
        for source in range(own_ref.shape[0]):
            own = own_ref[source].astype(jnp.float32)
            parts = [own[QUADS * k : QUADS * (k + 1)] for k in range(first_block, first_block + 4)]
            if first_block == 0:
                parts = [halo[0][source].astype(jnp.float32)[SB - QUADS :]] + parts
            else:
                parts = [own[QUADS * (first_block - 1) : QUADS * first_block]] + parts
            for k, part in enumerate(parts):
                wide_ref[QUADS * source : QUADS * (source + 1), 128 * k : 128 * (k + 1)] = part
        grid_ref[...] = wide_ref[...].astype(jnp.bfloat16)
        moved_ref[...] = pltpu.roll(wide_ref[...], 1, axis=0).astype(jnp.bfloat16)
        for t in range(3):
            first_row(t)
        for load in loads:
            load.wait()
        second_row(0)

    for row in range(1, 4):

        @pl.when(step == row)
        def _(row=row):
            first_row(2 * row + 1)
            first_row(2 * row + 2)
            second_row(row)


def convolutions(part, flags, halo, own, weights1, bias1, weights2, bias2, whole):
    columns = QUADS * own.shape[0]
    full = lambda a: pl.BlockSpec(a.shape, lambda i, *_: (0,) * a.ndim)
    anywhere = pl.BlockSpec(memory_space=pl.ANY)
    operands = [own, *weights1, bias1, weights2, bias2]
    if part == 0:
        operands = [halo] + operands
    specs = [anywhere if a is weights2 else full(a) for a in operands]
    aliases = {}
    if whole is not None:
        aliases = {1 + len(operands): 0}
        operands.append(whole)
        specs.append(anywhere)
    return pl.pallas_call(
        functools.partial(conv_kernel, 4 * part),
        grid_spec=pltpu.PrefetchScalarGridSpec(
            num_scalar_prefetch=1,
            grid=(4,),
            in_specs=specs,
            out_specs=[
                pl.BlockSpec((1, columns, C2), lambda i, flags: (flags[0] * 8 + 4 * part + i, 0, 0)),
                pl.BlockSpec((1, columns, C2), lambda i, *_: (i, 0, 0)),
            ],
            scratch_shapes=[
                pltpu.VMEM((columns, 640), jnp.float32),
                pltpu.VMEM((columns, 640), jnp.bfloat16),
                pltpu.VMEM((columns, 640), jnp.bfloat16),
                pltpu.VMEM((5 * columns, 3 * C1), jnp.bfloat16),
                pltpu.VMEM((4 * columns, 3 * C1), jnp.bfloat16),
                pltpu.VMEM(weights2.shape, jnp.bfloat16),
                pltpu.SemaphoreType.DMA((3, 3)),
            ],
        ),
        out_shape=[
            jax.ShapeDtypeStruct((16, columns, C2), jnp.bfloat16),
            jax.ShapeDtypeStruct((4, columns, C2), jnp.bfloat16),
        ],
        input_output_aliases=aliases,
        cost_estimate=pl.CostEstimate(
            flops=9_000_000_000, transcendentals=1_800_000, bytes_accessed=12_000_000
        ),
        compiler_params=pltpu.CompilerParams(
            dimension_semantics=("arbitrary",), vmem_limit_bytes=(40 if part else 40) << 20
        ),
    )(flags, *operands)


def first_weights(embed_weight, conv1_weight):
    channels = conv1_weight.astype(jnp.float32)
    values = jnp.einsum(
        "vc,tco->tvo",
        embed_weight.astype(jnp.float32),
        channels[:, 1:],
        precision=lax.Precision.HIGHEST,
    )
    taps = jnp.concatenate([channels[:, :1], values, jnp.zeros_like(channels[:, :1])], axis=1)
    taps = (0.5 * taps).astype(jnp.bfloat16).reshape(3, 3, FEAT, C1)

    def placed(part, above, below, phase):
        pads = ((above, below), (phase, PHASES - phase - part.shape[1]), (0, 0), (0, 0))
        return jnp.pad(part, pads).reshape(-1, C1)

    odd = [placed(taps, above, below, 1) for above, below in ((1, 0), (3, 2))]
    even = [
        jnp.concatenate(
            [placed(taps[:, 1:], above, below, 0), placed(taps[:, :1], above, below, 3)], axis=0
        )
        for above, below in ((1, 0), (3, 2))
    ]
    return odd + even


def shards(
    obs_tiles,
    tile_block,
    tile_rows,
    embed_weight,
    conv1_weight,
    conv1_bias,
    conv2_weight,
    conv2_bias,
):
    n_lon = lax.axis_size("lon")
    n_lat = lax.axis_size("lat")
    core = lax.axis_index("lon") % 2

    leaving = leaving_tiles(obs_tiles[0], tile_block[0].T, tile_rows[0].T)
    arrived = lax.all_to_all(leaving, ("lat", "lon"), 0, 0, tiled=True)
    notes = arrived[:, 2 * CAP, 0, : 2 * CAP].astype(jnp.int32)

    own = lax.all_to_all(set_convolution(notes, arrived, n_lon), "lon", 0, 0, tiled=True)
    last = own[:, 8 * QUADS - SB :]
    south = [(z * n_lon + i, z * n_lon + i + 1) for z in range(n_lat) for i in range(0, n_lon, 2)]
    south += [(b, b + n_lon - 1) for _, b in south if b + n_lon < n_lat * n_lon]
    halo = lax.ppermute(last, ("lat", "lon"), south)

    weights1 = first_weights(embed_weight, conv1_weight)
    weights2 = conv2_weight.reshape(3, 3, C1, C2)[:, ::-1].reshape(3, 3 * C1, C2)
    top = jnp.where((lax.axis_index("lat") == 0) & (core == 0), 0, 1)
    pairs = [(i, i ^ 1) for i in range(n_lon)]
    whole = None
    swapped = []
    for part in (1, 0):
        flags = jnp.stack([core, top if part == 0 else jnp.ones_like(top)]).astype(jnp.int32)
        whole, half = convolutions(
            part,
            flags,
            halo,
            own,
            weights1,
            0.5 * conv1_bias[None],
            weights2,
            conv2_bias[None],
            whole,
        )
        swapped.append((part, lax.ppermute(half, "lon", pairs)))
    for part, rows in swapped:
        whole = lax.dynamic_update_slice_in_dim(whole, rows, (1 - core) * 8 + 4 * part, axis=0)
    return whole


def solution(mesh):
    placed = (
        P(("lat", "lon"), None, None, None, None),
        P(("lat", "lon"), None, None),
        P(("lat", "lon"), None, None),
        P(),
        P(),
        P(),
        P(),
        P(),
    )
    return jax.shard_map(
        shards, mesh=mesh, in_specs=placed, out_specs=P("lat", None, None), check_vma=False
    )
```

```python
import functools

import jax
import jax.numpy as jnp
from jax import lax
from jax.experimental import pallas as pl
from jax.experimental.pallas import tpu as pltpu
from jax.sharding import PartitionSpec as P

BX = 64
BY = 48
SB = 16
TILE = 256
CAP = 4
FEAT = 8
KEPT = 7
C1 = 256
C2 = 512
SUBS = 12
PHASES = 4
QUADS = BY // PHASES
ROW_LANES = PHASES * FEAT
FAR = 8192.0
ROOT_HALF_LOG2E = (0.5 * 1.4426950408889634) ** 0.5
SOURCES = 32


def iota(shape, axis):
    return lax.broadcasted_iota(jnp.int32, shape, axis)


def setconv_kernel(note_ref, tiles_ref, out_ref, *sums):
    step = pl.program_id(0)

    @pl.when(step == 0)
    def _():
        for total in sums:
            total[...] = jnp.zeros_like(total)

    row = iota((SB, 1), 0)
    lane = iota((1, TILE), 1)
    center_row = (row.astype(jnp.float32) + 0.5) * ROOT_HALF_LOG2E
    center_col = ((row % 4 * 4 + row // 4).astype(jnp.float32) + 0.5) * ROOT_HALF_LOG2E

    def add_tile(source, slot, total):
        tile = jnp.concatenate([tiles_ref[source, slot], tiles_ref[source, slot + CAP]], axis=1)
        place = tile.astype(jnp.float32)
        live = lane < note_ref[step * SOURCES + source, CAP + slot]
        place_row = jnp.where(live, place[0:1], FAR)
        off_row = center_row - place_row * ROOT_HALF_LOG2E
        off_col = center_col - place[1:2] * ROOT_HALF_LOG2E
        along_row = jnp.exp2(-(off_row * off_row)).astype(jnp.bfloat16)
        along_col = jnp.exp2(-(off_col * off_col)).astype(jnp.bfloat16)
        weighted = [along_row]
        weighted += [tile[k : k + 1] * along_row for k in range(2, FEAT)]
        part = lax.dot_general(
            along_col,
            jnp.concatenate(weighted, axis=0),
            (((1,), (1,)), ((), ())),
            preferred_element_type=jnp.float32,
        )
        sub = note_ref[step * SOURCES + source, slot]
        total[sub] = total[sub] + part

    for k in range(SOURCES):
        for slot in range(CAP):
            add_tile(k, slot, sums[slot])

    @pl.when(step == pl.num_programs(0) - 1)
    def _():
        total = sums[0][...]
        for more in sums[1:]:
            total = total + more[...]
        total = total.reshape(SUBS * SB, KEPT * SB)
        total = jnp.concatenate([total, jnp.zeros((SUBS * SB, SB), jnp.float32)], axis=1)
        pick = (iota((128, 128), 0) == iota((128, 128), 1) % SB).astype(jnp.float32)
        density = jnp.dot(
            total, pick, precision=lax.Precision.HIGHEST, preferred_element_type=jnp.float32
        )
        lane = iota((SUBS * SB, 128), 1)
        grid = jnp.where(lane < SB, jnp.log1p(density), total / (1.0 + density))
        grid = grid.astype(jnp.bfloat16)
        target = iota((4 * SB, SUBS * SB), 0)
        source = iota((4 * SB, SUBS * SB), 1)
        quad = target % SB
        wanted = target // SB * BY + quad // 4 * SB + quad % 4
        parts = []
        for phase in range(PHASES):
            take = ((quad < QUADS) & (source == wanted + 4 * phase)).astype(jnp.bfloat16)
            parts.append(
                jnp.dot(take, grid, preferred_element_type=jnp.float32).astype(jnp.bfloat16)
            )
        spread = jnp.concatenate(parts, axis=1)
        lane_in = iota((512, 512), 0)
        lane_out = iota((512, 512), 1)
        moved = (
            lane_in % SB * ROW_LANES + lane_in // 128 * FEAT + lane_in % 128 // SB == lane_out
        ).astype(jnp.bfloat16)
        ordered = jnp.dot(spread, moved, preferred_element_type=jnp.float32).astype(jnp.bfloat16)
        to = iota((8 * QUADS, 4 * SB), 0)
        start = iota((8 * QUADS, 4 * SB), 1)
        for half in range(2):
            rows = None
            for k in range(4):
                take = (to // QUADS % 4 == k) & (
                    start == (2 * half + to // (4 * QUADS)) * SB + to % QUADS
                )
                part = jnp.dot(
                    take.astype(jnp.bfloat16),
                    ordered[:, 128 * k : 128 * k + 128],
                    preferred_element_type=jnp.float32,
                )
                rows = part if rows is None else rows + part
            rows = rows.astype(jnp.bfloat16)
            for k in range(out_ref.shape[0] // 2):
                out_ref[2 * k + half] = rows


def set_convolution(notes, arrived, copies):
    out = jax.ShapeDtypeStruct((copies, 8 * QUADS, 128), jnp.bfloat16)
    return pl.pallas_call(
        setconv_kernel,
        grid_spec=pltpu.PrefetchScalarGridSpec(
            num_scalar_prefetch=1,
            grid=(arrived.shape[0] // SOURCES,),
            in_specs=[pl.BlockSpec((SOURCES,) + arrived.shape[1:], lambda i, *_: (i, 0, 0, 0))],
            out_specs=pl.BlockSpec(out.shape, lambda i, *_: (0, 0, 0)),
            scratch_shapes=[pltpu.VMEM((SUBS, SB, KEPT * SB), jnp.float32)] * CAP,
        ),
        out_shape=out,
        compiler_params=pltpu.CompilerParams(
            dimension_semantics=("arbitrary",), vmem_limit_bytes=24 << 20
        ),
    )(notes, arrived)


def leave_kernel(sub_ref, rows_ref, tiles_ref, out_ref, notes_ref):
    step = pl.program_id(0)
    count = tiles_ref.shape[0]

    @pl.when(step == 0)
    def _():
        both = jnp.concatenate([sub_ref[...], rows_ref[...]], axis=0).astype(jnp.float32)
        blank = jnp.zeros((128 - 2 * CAP, both.shape[1]), jnp.float32)
        notes_ref[...] = jnp.concatenate([both, blank], axis=0).T

    notes = notes_ref[pl.ds(step * count, count), :]
    notes = jnp.broadcast_to(notes[:, None, :], (count, FEAT, 128)).astype(jnp.bfloat16)
    out_ref[:, :CAP] = tiles_ref[:, :, :, :128]
    out_ref[:, CAP : 2 * CAP] = tiles_ref[:, :, :, 128:]
    out_ref[:, 2 * CAP] = notes


def leaving_tiles(tiles, subs, rows):
    count = tiles.shape[0]
    part = count // 2
    return pl.pallas_call(
        leave_kernel,
        grid=(2,),
        in_specs=[
            pl.BlockSpec(subs.shape, lambda i: (0, 0)),
            pl.BlockSpec(rows.shape, lambda i: (0, 0)),
            pl.BlockSpec((part,) + tiles.shape[1:], lambda i: (i, 0, 0, 0)),
        ],
        out_specs=pl.BlockSpec((part, 2 * CAP + 1, FEAT, 128), lambda i: (i, 0, 0, 0)),
        out_shape=jax.ShapeDtypeStruct((count, 2 * CAP + 1, FEAT, 128), jnp.bfloat16),
        scratch_shapes=[pltpu.VMEM((count, 128), jnp.float32)],
        compiler_params=pltpu.CompilerParams(vmem_limit_bytes=60 << 20),
    )(subs, rows, tiles)


def placed(params, count, above, shift, low, high):
    lane = iota((count, params.shape[0]), 0)
    row_tap = lane // ROW_LANES - above
    col_tap = lane // FEAT % PHASES + shift
    wanted = (3 * row_tap + col_tap) * FEAT + lane % FEAT
    inside = (row_tap >= 0) & (row_tap < 3) & (col_tap >= low) & (col_tap < high)
    take = (inside & (iota(lane.shape, 1) == wanted)).astype(jnp.bfloat16)
    return jnp.dot(take, params, preferred_element_type=jnp.float32).astype(jnp.bfloat16)


def conv_kernel(first_block, *refs):
    flag_ref, *halo, own_ref, params_ref, weight2_hbm = refs[: 4 + (first_block == 0)]
    (out_ref, send_ref, wide_ref, grid_ref, moved_ref, even_rows, odd_rows, weight2_ref, odd1_ref,
     odd2_ref, even1_ref, even2_ref, sem) = refs[-13:]
    bias1 = params_ref[9 * FEAT : 9 * FEAT + 1, :]
    bias2 = jnp.concatenate(
        [params_ref[9 * FEAT + 1 : 9 * FEAT + 2, :], params_ref[9 * FEAT + 2 : 9 * FEAT + 3, :]],
        axis=1,
    )
    step = pl.program_id(0)
    columns = grid_ref.shape[0]
    loads = [
        pltpu.make_async_copy(
            weight2_hbm.at[tap, pl.ds(C1 * k, C1)], weight2_ref.at[tap, pl.ds(C1 * k, C1)], sem.at[tap, k]
        )
        for tap in range(3)
        for k in range(3)
    ]

    def first_row(t):
        block = t // 2
        if t % 2 == 0:
            here = grid_ref[:, 128 * block : 128 * block + 128]
            left = moved_ref[:, 128 * block : 128 * block + 128]
            odd = jnp.dot(here, odd1_ref[...], preferred_element_type=jnp.float32)
            weights = even1_ref
        else:
            here = grid_ref[:, 128 * block : 128 * block + 256]
            left = moved_ref[:, 128 * block : 128 * block + 256]
            odd = jnp.dot(here, odd2_ref[...], preferred_element_type=jnp.float32)
            weights = even2_ref
        even = jnp.dot(
            jnp.concatenate([here, left], axis=1), weights[...], preferred_element_type=jnp.float32
        )

        def activate(half):
            half = half + bias1
            return half * jnp.tanh(half) + half

        odd = activate(odd)
        even = activate(even)
        if t == 0:
            live = flag_ref[1].astype(jnp.float32)
            odd = odd * live
            even = even * live
        before = pltpu.roll(odd, 1, axis=0)
        store = even_rows if t % 2 == 0 else odd_rows
        at = pl.ds(block * columns, columns)
        store[at, 0:C1] = odd.astype(jnp.bfloat16)
        store[at, C1 : 2 * C1] = even.astype(jnp.bfloat16)
        store[at, 2 * C1 :] = before.astype(jnp.bfloat16)

    def second_row(row):
        total = None
        for tap, (store, at) in enumerate(
            [(even_rows, row), (odd_rows, row), (even_rows, row + 1)]
        ):
            part = jnp.dot(
                store[at * columns : (at + 1) * columns, :],
                weight2_ref[tap],
                preferred_element_type=jnp.float32,
            )
            total = part if total is None else total + part
        total = (total + bias2).astype(jnp.bfloat16).reshape(out_ref.shape)
        out_ref[...] = total
        send_ref[...] = total

    @pl.when(step == 0)
    def _():
        for load in loads:
            load.start()
        params = params_ref[...].astype(jnp.bfloat16)
        odd1_ref[...] = placed(params, 128, 1, -1, 0, 3)
        odd2_ref[...] = placed(params, 256, 3, -1, 0, 3)
        even1_ref[0:128, :] = placed(params, 128, 1, 1, 1, 3)
        even1_ref[128:256, :] = placed(params, 128, 1, -3, 0, 1)
        even2_ref[0:256, :] = placed(params, 256, 3, 1, 1, 3)
        even2_ref[256:512, :] = placed(params, 256, 3, -3, 0, 1)
        for source in range(own_ref.shape[0]):
            own = own_ref[source].astype(jnp.float32)
            parts = [own[QUADS * k : QUADS * (k + 1)] for k in range(first_block, first_block + 4)]
            if first_block == 0:
                parts = [halo[0][source].astype(jnp.float32)[SB - QUADS :]] + parts
            else:
                parts = [own[QUADS * (first_block - 1) : QUADS * first_block]] + parts
            for k, part in enumerate(parts):
                wide_ref[QUADS * source : QUADS * (source + 1), 128 * k : 128 * (k + 1)] = part
        grid_ref[...] = wide_ref[...].astype(jnp.bfloat16)
        moved_ref[...] = pltpu.roll(wide_ref[...], 1, axis=0).astype(jnp.bfloat16)
        for t in range(3):
            first_row(t)
        for load in loads:
            load.wait()
        second_row(0)

    for row in range(1, 4):

        @pl.when(step == row)
        def _(row=row):
            first_row(2 * row + 1)
            first_row(2 * row + 2)
            second_row(row)


def convolutions(part, flags, halo, own, params, weights2, whole):
    columns = QUADS * own.shape[0]
    full = lambda a: pl.BlockSpec(a.shape, lambda i, *_: (0,) * a.ndim)
    anywhere = pl.BlockSpec(memory_space=pl.ANY)
    operands = [own, params, weights2]
    if part == 0:
        operands = [halo] + operands
    specs = [anywhere if a is weights2 else full(a) for a in operands]
    aliases = {}
    if whole is not None:
        aliases = {1 + len(operands): 0}
        operands.append(whole)
        specs.append(anywhere)
    return pl.pallas_call(
        functools.partial(conv_kernel, 4 * part),
        grid_spec=pltpu.PrefetchScalarGridSpec(
            num_scalar_prefetch=1,
            grid=(4,),
            in_specs=specs,
            out_specs=[
                pl.BlockSpec((1, columns, C2), lambda i, flags: (flags[0] * 8 + 4 * part + i, 0, 0)),
                pl.BlockSpec((1, columns, C2), lambda i, *_: (i, 0, 0)),
            ],
            scratch_shapes=[
                pltpu.VMEM((columns, 640), jnp.float32),
                pltpu.VMEM((columns, 640), jnp.bfloat16),
                pltpu.VMEM((columns, 640), jnp.bfloat16),
                pltpu.VMEM((5 * columns, 3 * C1), jnp.bfloat16),
                pltpu.VMEM((4 * columns, 3 * C1), jnp.bfloat16),
                pltpu.VMEM(weights2.shape, jnp.bfloat16),
                pltpu.VMEM((128, C1), jnp.bfloat16),
                pltpu.VMEM((256, C1), jnp.bfloat16),
                pltpu.VMEM((256, C1), jnp.bfloat16),
                pltpu.VMEM((512, C1), jnp.bfloat16),
                pltpu.SemaphoreType.DMA((3, 3)),
            ],
        ),
        out_shape=[
            jax.ShapeDtypeStruct((16, columns, C2), jnp.bfloat16),
            jax.ShapeDtypeStruct((4, columns, C2), jnp.bfloat16),
        ],
        input_output_aliases=aliases,
        cost_estimate=pl.CostEstimate(
            flops=9_000_000_000, transcendentals=1_800_000, bytes_accessed=12_000_000
        ),
        compiler_params=pltpu.CompilerParams(
            dimension_semantics=("arbitrary",), vmem_limit_bytes=(40 if part else 40) << 20
        ),
    )(flags, *operands)


def first_weights(embed_weight, conv1_weight):
    channels = conv1_weight.astype(jnp.float32)
    values = jnp.einsum(
        "vc,tco->tvo",
        embed_weight.astype(jnp.float32),
        channels[:, 1:],
        precision=lax.Precision.HIGHEST,
    )
    taps = jnp.concatenate([channels[:, :1], values, jnp.zeros_like(channels[:, :1])], axis=1)
    return 0.5 * taps.reshape(9 * FEAT, C1)


def shards(
    obs_tiles,
    tile_block,
    tile_rows,
    embed_weight,
    conv1_weight,
    conv1_bias,
    conv2_weight,
    conv2_bias,
):
    n_lon = lax.axis_size("lon")
    n_lat = lax.axis_size("lat")
    core = lax.axis_index("lon") % 2

    leaving = leaving_tiles(obs_tiles[0], tile_block[0].T, tile_rows[0].T)
    arrived = lax.all_to_all(leaving, ("lat", "lon"), 0, 0, tiled=True)
    notes = arrived[:, 2 * CAP, 0, : 2 * CAP].astype(jnp.int32)

    halves = set_convolution(notes, arrived, n_lon)
    halves, conv2_weight = lax.optimization_barrier((halves, conv2_weight))
    own = lax.all_to_all(halves, "lon", 0, 0, tiled=True)
    last = own[:, 8 * QUADS - SB :]
    south = [(z * n_lon + i, z * n_lon + i + 1) for z in range(n_lat) for i in range(0, n_lon, 2)]
    south += [(b, b + n_lon - 1) for _, b in south if b + n_lon < n_lat * n_lon]
    halo = lax.ppermute(last, ("lat", "lon"), south)

    params = jnp.concatenate(
        [
            first_weights(embed_weight, conv1_weight),
            0.5 * conv1_bias[None],
            conv2_bias.reshape(2, C1),
            jnp.zeros((5, C1), jnp.float32),
        ],
        axis=0,
    )
    weights2 = conv2_weight.reshape(3, 3, C1, C2)[:, ::-1].reshape(3, 3 * C1, C2)
    top = jnp.where((lax.axis_index("lat") == 0) & (core == 0), 0, 1)
    pairs = [(i, i ^ 1) for i in range(n_lon)]
    whole = None
    swapped = []
    for part in (1, 0):
        flags = jnp.stack([core, top if part == 0 else jnp.ones_like(top)]).astype(jnp.int32)
        whole, half = convolutions(
            part,
            flags,
            halo,
            own,
            params,
            weights2,
            whole,
        )
        swapped.append((part, lax.ppermute(half, "lon", pairs)))
    for part, rows in swapped:
        whole = lax.dynamic_update_slice_in_dim(whole, rows, (1 - core) * 8 + 4 * part, axis=0)
    return whole


def solution(mesh):
    placed = (
        P(("lat", "lon"), None, None, None, None),
        P(("lat", "lon"), None, None),
        P(("lat", "lon"), None, None),
        P(),
        P(),
        P(),
        P(),
        P(),
    )
    return jax.shard_map(
        shards, mesh=mesh, in_specs=placed, out_specs=P("lat", None, None), check_vma=False
    )
```

```python
import functools

import jax
import jax.numpy as jnp
from jax import lax
from jax.experimental import pallas as pl
from jax.experimental.pallas import tpu as pltpu
from jax.sharding import PartitionSpec as P

BX = 64
BY = 48
SB = 16
TILE = 256
CAP = 4
FEAT = 8
KEPT = 7
C1 = 256
C2 = 512
SUBS = 12
PHASES = 4
QUADS = BY // PHASES
ROW_LANES = PHASES * FEAT
FAR = 8192.0
ROOT_HALF_LOG2E = (0.5 * 1.4426950408889634) ** 0.5
SOURCES = 32


def iota(shape, axis):
    return lax.broadcasted_iota(jnp.int32, shape, axis)


def setconv_kernel(note_ref, place_ref, tiles_ref, out_ref, *sums):
    step = pl.program_id(0)

    def note_row(source):
        index = (place_ref[0] - step + 4) % 4
        for axis, at in ((1, source // 8), (2, source // 2 % 4)):
            index = index * 4 + (place_ref[axis] - at + 4) % 4
        return index * 2 + (place_ref[3] - source % 2 + 2) % 2

    @pl.when(step == 0)
    def _():
        for total in sums:
            total[...] = jnp.zeros_like(total)

    row = iota((SB, 1), 0)
    lane = iota((1, TILE), 1)
    center_row = (row.astype(jnp.float32) + 0.5) * ROOT_HALF_LOG2E
    center_col = ((row % 4 * 4 + row // 4).astype(jnp.float32) + 0.5) * ROOT_HALF_LOG2E

    def add_tile(source, slot, note, total):
        tile = tiles_ref[source, slot]
        place = tile.astype(jnp.float32)
        live = lane < note_ref[note, CAP + slot]
        place_row = jnp.where(live, place[0:1], FAR)
        off_row = center_row - place_row * ROOT_HALF_LOG2E
        off_col = center_col - place[1:2] * ROOT_HALF_LOG2E
        along_row = jnp.exp2(-(off_row * off_row)).astype(jnp.bfloat16)
        along_col = jnp.exp2(-(off_col * off_col)).astype(jnp.bfloat16)
        weighted = [along_row]
        weighted += [tile[k : k + 1] * along_row for k in range(2, FEAT)]
        part = lax.dot_general(
            along_col,
            jnp.concatenate(weighted, axis=0),
            (((1,), (1,)), ((), ())),
            preferred_element_type=jnp.float32,
        )
        sub = note_ref[note, slot]
        total[sub] = total[sub] + part

    for k in range(SOURCES):
        note = note_row(k)
        for slot in range(CAP):
            add_tile(k, slot, note, sums[slot])

    @pl.when(step == pl.num_programs(0) - 1)
    def _():
        total = sums[0][...]
        for more in sums[1:]:
            total = total + more[...]
        total = total.reshape(SUBS * SB, KEPT * SB)
        total = jnp.concatenate([total, jnp.zeros((SUBS * SB, SB), jnp.float32)], axis=1)
        pick = (iota((128, 128), 0) == iota((128, 128), 1) % SB).astype(jnp.float32)
        density = jnp.dot(
            total, pick, precision=lax.Precision.HIGHEST, preferred_element_type=jnp.float32
        )
        lane = iota((SUBS * SB, 128), 1)
        grid = jnp.where(lane < SB, jnp.log1p(density), total / (1.0 + density))
        grid = grid.astype(jnp.bfloat16)
        target = iota((4 * SB, SUBS * SB), 0)
        source = iota((4 * SB, SUBS * SB), 1)
        quad = target % SB
        wanted = target // SB * BY + quad // 4 * SB + quad % 4
        parts = []
        for phase in range(PHASES):
            take = ((quad < QUADS) & (source == wanted + 4 * phase)).astype(jnp.bfloat16)
            parts.append(
                jnp.dot(take, grid, preferred_element_type=jnp.float32).astype(jnp.bfloat16)
            )
        spread = jnp.concatenate(parts, axis=1)
        lane_in = iota((512, 512), 0)
        lane_out = iota((512, 512), 1)
        moved = (
            lane_in % SB * ROW_LANES + lane_in // 128 * FEAT + lane_in % 128 // SB == lane_out
        ).astype(jnp.bfloat16)
        ordered = jnp.dot(spread, moved, preferred_element_type=jnp.float32).astype(jnp.bfloat16)
        to = iota((8 * QUADS, 4 * SB), 0)
        start = iota((8 * QUADS, 4 * SB), 1)
        for half in range(2):
            rows = None
            for k in range(4):
                take = (to // QUADS % 4 == k) & (
                    start == (2 * half + to // (4 * QUADS)) * SB + to % QUADS
                )
                part = jnp.dot(
                    take.astype(jnp.bfloat16),
                    ordered[:, 128 * k : 128 * k + 128],
                    preferred_element_type=jnp.float32,
                )
                rows = part if rows is None else rows + part
            rows = rows.astype(jnp.bfloat16)
            for k in range(out_ref.shape[0] // 2):
                out_ref[2 * k + half] = rows


def set_convolution(notes, place, arrived, copies):
    out = jax.ShapeDtypeStruct((copies, 8 * QUADS, 128), jnp.bfloat16)
    return pl.pallas_call(
        setconv_kernel,
        grid_spec=pltpu.PrefetchScalarGridSpec(
            num_scalar_prefetch=2,
            grid=(arrived.shape[0] // SOURCES,),
            in_specs=[pl.BlockSpec((SOURCES,) + arrived.shape[1:], lambda i, *_: (i, 0, 0, 0))],
            out_specs=pl.BlockSpec(out.shape, lambda i, *_: (0, 0, 0)),
            scratch_shapes=[pltpu.VMEM((SUBS, SB, KEPT * SB), jnp.float32)] * CAP,
        ),
        out_shape=out,
        compiler_params=pltpu.CompilerParams(
            dimension_semantics=("arbitrary",), vmem_limit_bytes=24 << 20
        ),
    )(notes, place, arrived)


def placed(params, count, above, shift, low, high):
    lane = iota((count, params.shape[0]), 0)
    row_tap = lane // ROW_LANES - above
    col_tap = lane // FEAT % PHASES + shift
    wanted = (3 * row_tap + col_tap) * FEAT + lane % FEAT
    inside = (row_tap >= 0) & (row_tap < 3) & (col_tap >= low) & (col_tap < high)
    take = (inside & (iota(lane.shape, 1) == wanted)).astype(jnp.bfloat16)
    return jnp.dot(take, params, preferred_element_type=jnp.float32).astype(jnp.bfloat16)


def conv_kernel(first_block, *refs):
    flag_ref, *halo, own_ref, params_ref, weight2_hbm = refs[: 4 + (first_block == 0)]
    (out_ref, send_ref, wide_ref, grid_ref, moved_ref, even_rows, odd_rows, weight2_ref, odd1_ref,
     odd2_ref, even1_ref, even2_ref, sem) = refs[-13:]
    bias1 = params_ref[9 * FEAT : 9 * FEAT + 1, :]
    bias2 = jnp.concatenate(
        [params_ref[9 * FEAT + 1 : 9 * FEAT + 2, :], params_ref[9 * FEAT + 2 : 9 * FEAT + 3, :]],
        axis=1,
    )
    step = pl.program_id(0)
    columns = grid_ref.shape[0]
    loads = [
        pltpu.make_async_copy(
            weight2_hbm.at[tap, pl.ds(C1 * k, C1)], weight2_ref.at[tap, pl.ds(C1 * k, C1)], sem.at[tap, k]
        )
        for tap in range(3)
        for k in range(3)
    ]

    def first_row(t):
        block = t // 2
        if t % 2 == 0:
            here = grid_ref[:, 128 * block : 128 * block + 128]
            left = moved_ref[:, 128 * block : 128 * block + 128]
            odd = jnp.dot(here, odd1_ref[...], preferred_element_type=jnp.float32)
            weights = even1_ref
        else:
            here = grid_ref[:, 128 * block : 128 * block + 256]
            left = moved_ref[:, 128 * block : 128 * block + 256]
            odd = jnp.dot(here, odd2_ref[...], preferred_element_type=jnp.float32)
            weights = even2_ref
        even = jnp.dot(
            jnp.concatenate([here, left], axis=1), weights[...], preferred_element_type=jnp.float32
        )

        def activate(half):
            half = half + bias1
            return half * jnp.tanh(half) + half

        odd = activate(odd)
        even = activate(even)
        if t == 0:
            live = flag_ref[1].astype(jnp.float32)
            odd = odd * live
            even = even * live
        before = pltpu.roll(odd, 1, axis=0)
        store = even_rows if t % 2 == 0 else odd_rows
        at = pl.ds(block * columns, columns)
        store[at, 0:C1] = odd.astype(jnp.bfloat16)
        store[at, C1 : 2 * C1] = even.astype(jnp.bfloat16)
        store[at, 2 * C1 :] = before.astype(jnp.bfloat16)

    def second_row(row):
        total = None
        for tap, (store, at) in enumerate(
            [(even_rows, row), (odd_rows, row), (even_rows, row + 1)]
        ):
            part = jnp.dot(
                store[at * columns : (at + 1) * columns, :],
                weight2_ref[tap],
                preferred_element_type=jnp.float32,
            )
            total = part if total is None else total + part
        total = (total + bias2).astype(jnp.bfloat16).reshape(out_ref.shape)
        out_ref[...] = total
        send_ref[...] = total

    @pl.when(step == 0)
    def _():
        for load in loads:
            load.start()
        params = params_ref[...].astype(jnp.bfloat16)
        odd1_ref[...] = placed(params, 128, 1, -1, 0, 3)
        odd2_ref[...] = placed(params, 256, 3, -1, 0, 3)
        even1_ref[0:128, :] = placed(params, 128, 1, 1, 1, 3)
        even1_ref[128:256, :] = placed(params, 128, 1, -3, 0, 1)
        even2_ref[0:256, :] = placed(params, 256, 3, 1, 1, 3)
        even2_ref[256:512, :] = placed(params, 256, 3, -3, 0, 1)
        for source in range(own_ref.shape[0]):
            own = own_ref[source].astype(jnp.float32)
            parts = [own[QUADS * k : QUADS * (k + 1)] for k in range(first_block, first_block + 4)]
            if first_block == 0:
                parts = [halo[0][source].astype(jnp.float32)[SB - QUADS :]] + parts
            else:
                parts = [own[QUADS * (first_block - 1) : QUADS * first_block]] + parts
            for k, part in enumerate(parts):
                wide_ref[QUADS * source : QUADS * (source + 1), 128 * k : 128 * (k + 1)] = part
        grid_ref[...] = wide_ref[...].astype(jnp.bfloat16)
        moved_ref[...] = pltpu.roll(wide_ref[...], 1, axis=0).astype(jnp.bfloat16)
        for t in range(3):
            first_row(t)
        for load in loads:
            load.wait()
        second_row(0)

    for row in range(1, 4):

        @pl.when(step == row)
        def _(row=row):
            first_row(2 * row + 1)
            first_row(2 * row + 2)
            second_row(row)


def convolutions(part, flags, halo, own, params, weights2, whole):
    columns = QUADS * own.shape[0]
    full = lambda a: pl.BlockSpec(a.shape, lambda i, *_: (0,) * a.ndim)
    anywhere = pl.BlockSpec(memory_space=pl.ANY)
    operands = [own, params, weights2]
    if part == 0:
        operands = [halo] + operands
    specs = [anywhere if a is weights2 else full(a) for a in operands]
    aliases = {}
    if whole is not None:
        aliases = {1 + len(operands): 0}
        operands.append(whole)
        specs.append(anywhere)
    return pl.pallas_call(
        functools.partial(conv_kernel, 4 * part),
        grid_spec=pltpu.PrefetchScalarGridSpec(
            num_scalar_prefetch=1,
            grid=(4,),
            in_specs=specs,
            out_specs=[
                pl.BlockSpec((1, columns, C2), lambda i, flags: (flags[0] * 8 + 4 * part + i, 0, 0)),
                pl.BlockSpec((1, columns, C2), lambda i, *_: (i, 0, 0)),
            ],
            scratch_shapes=[
                pltpu.VMEM((columns, 640), jnp.float32),
                pltpu.VMEM((columns, 640), jnp.bfloat16),
                pltpu.VMEM((columns, 640), jnp.bfloat16),
                pltpu.VMEM((5 * columns, 3 * C1), jnp.bfloat16),
                pltpu.VMEM((4 * columns, 3 * C1), jnp.bfloat16),
                pltpu.VMEM(weights2.shape, jnp.bfloat16),
                pltpu.VMEM((128, C1), jnp.bfloat16),
                pltpu.VMEM((256, C1), jnp.bfloat16),
                pltpu.VMEM((256, C1), jnp.bfloat16),
                pltpu.VMEM((512, C1), jnp.bfloat16),
                pltpu.SemaphoreType.DMA((3, 3)),
            ],
        ),
        out_shape=[
            jax.ShapeDtypeStruct((16, columns, C2), jnp.bfloat16),
            jax.ShapeDtypeStruct((4, columns, C2), jnp.bfloat16),
        ],
        input_output_aliases=aliases,
        cost_estimate=pl.CostEstimate(
            flops=9_000_000_000, transcendentals=1_800_000, bytes_accessed=12_000_000
        ),
        compiler_params=pltpu.CompilerParams(
            dimension_semantics=("arbitrary",), vmem_limit_bytes=(40 if part else 40) << 20
        ),
    )(flags, *operands)


def first_weights(embed_weight, conv1_weight):
    channels = conv1_weight.astype(jnp.float32)
    values = jnp.einsum(
        "vc,tco->tvo",
        embed_weight.astype(jnp.float32),
        channels[:, 1:],
        precision=lax.Precision.HIGHEST,
    )
    taps = jnp.concatenate([channels[:, :1], values, jnp.zeros_like(channels[:, :1])], axis=1)
    return 0.5 * taps.reshape(9 * FEAT, C1)


def shards(
    obs_tiles,
    tile_block,
    tile_rows,
    embed_weight,
    conv1_weight,
    conv1_bias,
    conv2_weight,
    conv2_bias,
):
    n_lon = lax.axis_size("lon")
    n_lat = lax.axis_size("lat")
    core = lax.axis_index("lon") % 2

    arrived = lax.all_to_all(obs_tiles[0], ("lat", "lon"), 0, 0, tiled=True)

    lon = lax.axis_index("lon")
    place = [lax.axis_index("lat"), lon // 8, lon // 2 % 4, core]
    notes = jnp.concatenate([tile_block[0], tile_rows[0]], axis=1).astype(jnp.bfloat16)
    notes = notes.reshape(4, 4, 4, 2, 2 * CAP)
    for axis, at in enumerate(place):
        size = notes.shape[axis]
        notes = lax.dynamic_slice_in_dim(
            jnp.concatenate([notes, notes], axis=axis), at, size, axis=axis
        )

    def ahead(i, axis, k):
        if axis == 1:
            return (i + 8 * k) % n_lon
        if axis == 2:
            return i // 8 * 8 + (i + 2 * k) % 8
        return i ^ k

    for axis in range(4):
        parts = [lax.index_in_dim(notes, k, axis) for k in range(notes.shape[axis])]
        for k in range(1, len(parts)):
            if axis == 0:
                parts[k] = lax.ppermute(parts[k], "lat", [(i, (i + k) % n_lat) for i in range(n_lat)])
            else:
                parts[k] = lax.ppermute(
                    parts[k], "lon", [(i, ahead(i, axis, k)) for i in range(n_lon)]
                )
        notes = jnp.concatenate(parts, axis=axis)
    notes = notes.reshape(-1, 2 * CAP).astype(jnp.int32)

    halves = set_convolution(notes, jnp.stack(place).astype(jnp.int32), arrived, n_lon)
    halves, conv2_weight = lax.optimization_barrier((halves, conv2_weight))
    own = lax.all_to_all(halves, "lon", 0, 0, tiled=True)
    last = own[:, 8 * QUADS - SB :]
    south = [(z * n_lon + i, z * n_lon + i + 1) for z in range(n_lat) for i in range(0, n_lon, 2)]
    south += [(b, b + n_lon - 1) for _, b in south if b + n_lon < n_lat * n_lon]
    halo = lax.ppermute(last, ("lat", "lon"), south)

    params = jnp.concatenate(
        [
            first_weights(embed_weight, conv1_weight),
            0.5 * conv1_bias[None],
            conv2_bias.reshape(2, C1),
            jnp.zeros((5, C1), jnp.float32),
        ],
        axis=0,
    )
    weights2 = conv2_weight.reshape(3, 3, C1, C2)[:, ::-1].reshape(3, 3 * C1, C2)
    top = jnp.where((lax.axis_index("lat") == 0) & (core == 0), 0, 1)
    pairs = [(i, i ^ 1) for i in range(n_lon)]
    whole = None
    swapped = []
    for part in (1, 0):
        flags = jnp.stack([core, top if part == 0 else jnp.ones_like(top)]).astype(jnp.int32)
        whole, half = convolutions(
            part,
            flags,
            halo,
            own,
            params,
            weights2,
            whole,
        )
        swapped.append((part, lax.ppermute(half, "lon", pairs)))
    for part, rows in swapped:
        whole = lax.dynamic_update_slice_in_dim(whole, rows, (1 - core) * 8 + 4 * part, axis=0)
    return whole


def solution(mesh):
    placed = (
        P(("lat", "lon"), None, None, None, None),
        P(("lat", "lon"), None, None),
        P(("lat", "lon"), None, None),
        P(),
        P(),
        P(),
        P(),
        P(),
    )
    return jax.shard_map(
        shards, mesh=mesh, in_specs=placed, out_specs=P("lat", None, None), check_vma=False
    )
```

```python
import functools

import jax
import jax.numpy as jnp
from jax import lax
from jax.experimental import pallas as pl
from jax.experimental.pallas import tpu as pltpu
from jax.sharding import PartitionSpec as P

BX = 64
BY = 48
SB = 16
TILE = 256
CAP = 4
FEAT = 8
KEPT = 7
C1 = 256
C2 = 512
SUBS = 12
PHASES = 4
QUADS = BY // PHASES
ROW_LANES = PHASES * FEAT
FAR = 8192.0
ROOT_HALF_LOG2E = (0.5 * 1.4426950408889634) ** 0.5
SOURCES = 128


def iota(shape, axis):
    return lax.broadcasted_iota(jnp.int32, shape, axis)


def setconv_kernel(note_ref, tiles_ref, out_ref, *sums):
    step = pl.program_id(0)

    @pl.when(step == 0)
    def _():
        for total in sums:
            total[...] = jnp.zeros_like(total)

    row = iota((SB, 1), 0)
    lane = iota((1, TILE), 1)
    center_row = (row.astype(jnp.float32) + 0.5) * ROOT_HALF_LOG2E
    center_col = ((row % 4 * 4 + row // 4).astype(jnp.float32) + 0.5) * ROOT_HALF_LOG2E

    def add_tile(source, slot, total):
        tile = jnp.concatenate([tiles_ref[source, slot], tiles_ref[source, slot + CAP]], axis=1)
        place = tile.astype(jnp.float32)
        live = lane < note_ref[step * SOURCES + source, CAP + slot]
        place_row = jnp.where(live, place[0:1], FAR)
        off_row = center_row - place_row * ROOT_HALF_LOG2E
        off_col = center_col - place[1:2] * ROOT_HALF_LOG2E
        along_row = jnp.exp2(-(off_row * off_row)).astype(jnp.bfloat16)
        along_col = jnp.exp2(-(off_col * off_col)).astype(jnp.bfloat16)
        weighted = [along_row]
        weighted += [tile[k : k + 1] * along_row for k in range(2, FEAT)]
        part = lax.dot_general(
            along_col,
            jnp.concatenate(weighted, axis=0),
            (((1,), (1,)), ((), ())),
            preferred_element_type=jnp.float32,
        )
        sub = note_ref[step * SOURCES + source, slot]
        total[sub] = total[sub] + part

    for k in range(SOURCES):
        for slot in range(CAP):
            add_tile(k, slot, sums[slot])

    @pl.when(step == pl.num_programs(0) - 1)
    def _():
        total = sums[0][...]
        for more in sums[1:]:
            total = total + more[...]
        total = total.reshape(SUBS * SB, KEPT * SB)
        total = jnp.concatenate([total, jnp.zeros((SUBS * SB, SB), jnp.float32)], axis=1)
        lane = iota((SUBS * SB, 128), 1)
        density = jnp.where(lane < SB, total, 0.0)
        for places in (SB, 2 * SB, 4 * SB):
            density = density + pltpu.roll(density, places, axis=1)
        grid = jnp.where(lane < SB, jnp.log1p(density), total / (1.0 + density))
        grid = grid.astype(jnp.bfloat16)
        target = iota((4 * SB, 1), 0)
        source = iota((1, SUBS * SB), 1)
        quad = target & (SB - 1)
        wanted = (target >> 4) * BY + (quad >> 2) * SB + (quad & 3)
        wanted = jnp.where(quad < QUADS, wanted, -SUBS * SB)
        parts = []
        for phase in range(PHASES):
            take = (source == wanted + 4 * phase).astype(jnp.bfloat16)
            parts.append(
                jnp.dot(take, grid, preferred_element_type=jnp.float32).astype(jnp.bfloat16)
            )
        spread = jnp.concatenate(parts, axis=1)
        lane_in = iota((512, 1), 0)
        lane_out = (lane_in & 15) * ROW_LANES + (lane_in >> 7) * FEAT + ((lane_in & 127) >> 4)
        moved = (iota((1, 512), 1) == lane_out).astype(jnp.bfloat16)
        ordered = jnp.dot(spread, moved, preferred_element_type=jnp.float32).astype(jnp.bfloat16)
        to = iota((8 * QUADS, 1), 0)
        block = to // QUADS
        quad = to - block * QUADS
        start = iota((1, 4 * SB), 1)
        for half in range(2):
            rows = None
            for k in range(4):
                wanted = (2 * half + (block >> 2)) * SB + quad
                take = start == jnp.where((block & 3) == k, wanted, -1)
                part = jnp.dot(
                    take.astype(jnp.bfloat16),
                    ordered[:, 128 * k : 128 * k + 128],
                    preferred_element_type=jnp.float32,
                )
                rows = part if rows is None else rows + part
            rows = rows.astype(jnp.bfloat16)
            for k in range(out_ref.shape[0] // 2):
                out_ref[2 * k + half] = rows


def set_convolution(notes, arrived, copies):
    out = jax.ShapeDtypeStruct((copies, 8 * QUADS, 128), jnp.bfloat16)
    return pl.pallas_call(
        setconv_kernel,
        grid_spec=pltpu.PrefetchScalarGridSpec(
            num_scalar_prefetch=1,
            grid=(arrived.shape[0] // SOURCES,),
            in_specs=[pl.BlockSpec((SOURCES,) + arrived.shape[1:], lambda i, *_: (i, 0, 0, 0))],
            out_specs=pl.BlockSpec(out.shape, lambda i, *_: (0, 0, 0)),
            scratch_shapes=[pltpu.VMEM((SUBS, SB, KEPT * SB), jnp.float32)] * CAP,
        ),
        out_shape=out,
        compiler_params=pltpu.CompilerParams(
            dimension_semantics=("arbitrary",), vmem_limit_bytes=24 << 20
        ),
    )(notes, arrived)


def leave_kernel(sub_ref, rows_ref, tiles_ref, out_ref, notes_ref):
    step = pl.program_id(0)
    count = tiles_ref.shape[0]

    @pl.when(step == 0)
    def _():
        both = jnp.concatenate([sub_ref[...], rows_ref[...]], axis=0).astype(jnp.float32)
        blank = jnp.zeros((128 - 2 * CAP, both.shape[1]), jnp.float32)
        notes_ref[...] = jnp.concatenate([both, blank], axis=0).T

    notes = notes_ref[pl.ds(step * count, count), :]
    notes = jnp.broadcast_to(notes[:, None, :], (count, FEAT, 128)).astype(jnp.bfloat16)
    out_ref[:, :CAP] = tiles_ref[:, :, :, :128]
    out_ref[:, CAP : 2 * CAP] = tiles_ref[:, :, :, 128:]
    out_ref[:, 2 * CAP] = notes


def leaving_tiles(tiles, subs, rows):
    count = tiles.shape[0]
    part = count // 2
    return pl.pallas_call(
        leave_kernel,
        grid=(2,),
        in_specs=[
            pl.BlockSpec(subs.shape, lambda i: (0, 0)),
            pl.BlockSpec(rows.shape, lambda i: (0, 0)),
            pl.BlockSpec((part,) + tiles.shape[1:], lambda i: (i, 0, 0, 0)),
        ],
        out_specs=pl.BlockSpec((part, 2 * CAP + 1, FEAT, 128), lambda i: (i, 0, 0, 0)),
        out_shape=jax.ShapeDtypeStruct((count, 2 * CAP + 1, FEAT, 128), jnp.bfloat16),
        scratch_shapes=[pltpu.VMEM((count, 128), jnp.float32)],
        compiler_params=pltpu.CompilerParams(vmem_limit_bytes=60 << 20),
    )(subs, rows, tiles)


def placed(params, count, above, shift, low, high):
    lane = iota((count, params.shape[0]), 0)
    row_tap = lane // ROW_LANES - above
    col_tap = lane // FEAT % PHASES + shift
    wanted = (3 * row_tap + col_tap) * FEAT + lane % FEAT
    inside = (row_tap >= 0) & (row_tap < 3) & (col_tap >= low) & (col_tap < high)
    take = (inside & (iota(lane.shape, 1) == wanted)).astype(jnp.bfloat16)
    return jnp.dot(take, params, preferred_element_type=jnp.float32).astype(jnp.bfloat16)


def conv_kernel(first_block, *refs):
    flag_ref, *halo, own_ref, params_ref, weight2_hbm = refs[: 4 + (first_block == 0)]
    (out_ref, send_ref, wide_ref, grid_ref, moved_ref, even_rows, odd_rows, weight2_ref, odd1_ref,
     odd2_ref, even1_ref, even2_ref, sem) = refs[-13:]
    bias1 = params_ref[9 * FEAT : 9 * FEAT + 1, :]
    bias2 = jnp.concatenate(
        [params_ref[9 * FEAT + 1 : 9 * FEAT + 2, :], params_ref[9 * FEAT + 2 : 9 * FEAT + 3, :]],
        axis=1,
    )
    step = pl.program_id(0)
    columns = grid_ref.shape[0]
    loads = [
        pltpu.make_async_copy(
            weight2_hbm.at[tap, pl.ds(C1 * k, C1)], weight2_ref.at[tap, pl.ds(C1 * k, C1)], sem.at[tap, k]
        )
        for tap in range(3)
        for k in range(3)
    ]

    def first_row(t):
        block = t // 2
        if t % 2 == 0:
            here = grid_ref[:, 128 * block : 128 * block + 128]
            left = moved_ref[:, 128 * block : 128 * block + 128]
            odd = jnp.dot(here, odd1_ref[...], preferred_element_type=jnp.float32)
            weights = even1_ref
        else:
            here = grid_ref[:, 128 * block : 128 * block + 256]
            left = moved_ref[:, 128 * block : 128 * block + 256]
            odd = jnp.dot(here, odd2_ref[...], preferred_element_type=jnp.float32)
            weights = even2_ref
        even = jnp.dot(
            jnp.concatenate([here, left], axis=1), weights[...], preferred_element_type=jnp.float32
        )

        def activate(half):
            half = half + bias1
            return half * jnp.tanh(half) + half

        odd = activate(odd)
        even = activate(even)
        if t == 0:
            live = flag_ref[1].astype(jnp.float32)
            odd = odd * live
            even = even * live
        before = pltpu.roll(odd, 1, axis=0)
        store = even_rows if t % 2 == 0 else odd_rows
        at = pl.ds(block * columns, columns)
        store[at, 0:C1] = odd.astype(jnp.bfloat16)
        store[at, C1 : 2 * C1] = even.astype(jnp.bfloat16)
        store[at, 2 * C1 :] = before.astype(jnp.bfloat16)

    def second_row(row):
        total = None
        for tap, (store, at) in enumerate(
            [(even_rows, row), (odd_rows, row), (even_rows, row + 1)]
        ):
            part = jnp.dot(
                store[at * columns : (at + 1) * columns, :],
                weight2_ref[tap],
                preferred_element_type=jnp.float32,
            )
            total = part if total is None else total + part
        total = (total + bias2).astype(jnp.bfloat16).reshape(out_ref.shape)
        out_ref[...] = total
        send_ref[...] = total

    @pl.when(step == 0)
    def _():
        for load in loads:
            load.start()
        params = params_ref[...].astype(jnp.bfloat16)
        odd1_ref[...] = placed(params, 128, 1, -1, 0, 3)
        odd2_ref[...] = placed(params, 256, 3, -1, 0, 3)
        even1_ref[0:128, :] = placed(params, 128, 1, 1, 1, 3)
        even1_ref[128:256, :] = placed(params, 128, 1, -3, 0, 1)
        even2_ref[0:256, :] = placed(params, 256, 3, 1, 1, 3)
        even2_ref[256:512, :] = placed(params, 256, 3, -3, 0, 1)
        for source in range(own_ref.shape[0]):
            own = own_ref[source].astype(jnp.float32)
            parts = [own[QUADS * k : QUADS * (k + 1)] for k in range(first_block, first_block + 4)]
            if first_block == 0:
                parts = [halo[0][source].astype(jnp.float32)[SB - QUADS :]] + parts
            else:
                parts = [own[QUADS * (first_block - 1) : QUADS * first_block]] + parts
            for k, part in enumerate(parts):
                wide_ref[QUADS * source : QUADS * (source + 1), 128 * k : 128 * (k + 1)] = part
        grid_ref[...] = wide_ref[...].astype(jnp.bfloat16)
        moved_ref[...] = pltpu.roll(wide_ref[...], 1, axis=0).astype(jnp.bfloat16)
        for t in range(3):
            first_row(t)
        for load in loads:
            load.wait()
        second_row(0)

    for row in range(1, 4):

        @pl.when(step == row)
        def _(row=row):
            first_row(2 * row + 1)
            first_row(2 * row + 2)
            second_row(row)


def convolutions(part, flags, halo, own, params, weights2, whole):
    columns = QUADS * own.shape[0]
    full = lambda a: pl.BlockSpec(a.shape, lambda i, *_: (0,) * a.ndim)
    anywhere = pl.BlockSpec(memory_space=pl.ANY)
    operands = [own, params, weights2]
    if part == 0:
        operands = [halo] + operands
    specs = [anywhere if a is weights2 else full(a) for a in operands]
    aliases = {}
    if whole is not None:
        aliases = {1 + len(operands): 0}
        operands.append(whole)
        specs.append(anywhere)
    return pl.pallas_call(
        functools.partial(conv_kernel, 4 * part),
        grid_spec=pltpu.PrefetchScalarGridSpec(
            num_scalar_prefetch=1,
            grid=(4,),
            in_specs=specs,
            out_specs=[
                pl.BlockSpec((1, columns, C2), lambda i, flags: (flags[0] * 8 + 4 * part + i, 0, 0)),
                pl.BlockSpec((1, columns, C2), lambda i, *_: (i, 0, 0)),
            ],
            scratch_shapes=[
                pltpu.VMEM((columns, 640), jnp.float32),
                pltpu.VMEM((columns, 640), jnp.bfloat16),
                pltpu.VMEM((columns, 640), jnp.bfloat16),
                pltpu.VMEM((5 * columns, 3 * C1), jnp.bfloat16),
                pltpu.VMEM((4 * columns, 3 * C1), jnp.bfloat16),
                pltpu.VMEM(weights2.shape, jnp.bfloat16),
                pltpu.VMEM((128, C1), jnp.bfloat16),
                pltpu.VMEM((256, C1), jnp.bfloat16),
                pltpu.VMEM((256, C1), jnp.bfloat16),
                pltpu.VMEM((512, C1), jnp.bfloat16),
                pltpu.SemaphoreType.DMA((3, 3)),
            ],
        ),
        out_shape=[
            jax.ShapeDtypeStruct((16, columns, C2), jnp.bfloat16),
            jax.ShapeDtypeStruct((4, columns, C2), jnp.bfloat16),
        ],
        input_output_aliases=aliases,
        cost_estimate=pl.CostEstimate(
            flops=9_000_000_000, transcendentals=1_800_000, bytes_accessed=12_000_000
        ),
        compiler_params=pltpu.CompilerParams(
            dimension_semantics=("arbitrary",), vmem_limit_bytes=(40 if part else 40) << 20
        ),
    )(flags, *operands)


def first_weights(embed_weight, conv1_weight):
    channels = conv1_weight.astype(jnp.float32)
    values = jnp.einsum(
        "vc,tco->tvo",
        embed_weight.astype(jnp.float32),
        channels[:, 1:],
        precision=lax.Precision.HIGHEST,
    )
    taps = jnp.concatenate([channels[:, :1], values, jnp.zeros_like(channels[:, :1])], axis=1)
    return 0.5 * taps.reshape(9 * FEAT, C1)


def shards(
    obs_tiles,
    tile_block,
    tile_rows,
    embed_weight,
    conv1_weight,
    conv1_bias,
    conv2_weight,
    conv2_bias,
):
    n_lon = lax.axis_size("lon")
    n_lat = lax.axis_size("lat")
    core = lax.axis_index("lon") % 2

    leaving = leaving_tiles(obs_tiles[0], tile_block[0].T, tile_rows[0].T)
    arrived = lax.all_to_all(leaving, ("lat", "lon"), 0, 0, tiled=True)
    notes = arrived[:, 2 * CAP, 0, : 2 * CAP].astype(jnp.int32)

    halves = set_convolution(notes, arrived, n_lon)
    halves, conv2_weight = lax.optimization_barrier((halves, conv2_weight))
    own = lax.all_to_all(halves, "lon", 0, 0, tiled=True)
    last = own[:, 8 * QUADS - SB :]
    south = [(z * n_lon + i, z * n_lon + i + 1) for z in range(n_lat) for i in range(0, n_lon, 2)]
    south += [(b, b + n_lon - 1) for _, b in south if b + n_lon < n_lat * n_lon]
    halo = lax.ppermute(last, ("lat", "lon"), south)

    params = jnp.concatenate(
        [
            first_weights(embed_weight, conv1_weight),
            0.5 * conv1_bias[None],
            conv2_bias.reshape(2, C1),
            jnp.zeros((5, C1), jnp.float32),
        ],
        axis=0,
    )
    weights2 = conv2_weight.reshape(3, 3, C1, C2)[:, ::-1].reshape(3, 3 * C1, C2)
    top = jnp.where((lax.axis_index("lat") == 0) & (core == 0), 0, 1)
    pairs = [(i, i ^ 1) for i in range(n_lon)]
    whole = None
    swapped = []
    for part in (1, 0):
        flags = jnp.stack([core, top if part == 0 else jnp.ones_like(top)]).astype(jnp.int32)
        whole, half = convolutions(
            part,
            flags,
            halo,
            own,
            params,
            weights2,
            whole,
        )
        swapped.append((part, lax.ppermute(half, "lon", pairs)))
    for part, rows in swapped:
        whole = lax.dynamic_update_slice_in_dim(whole, rows, (1 - core) * 8 + 4 * part, axis=0)
    return whole


def solution(mesh):
    placed = (
        P(("lat", "lon"), None, None, None, None),
        P(("lat", "lon"), None, None),
        P(("lat", "lon"), None, None),
        P(),
        P(),
        P(),
        P(),
        P(),
    )
    return jax.shard_map(
        shards, mesh=mesh, in_specs=placed, out_specs=P("lat", None, None), check_vma=False
    )
```

```python
import functools

import jax
import jax.numpy as jnp
from jax import lax
from jax.experimental import pallas as pl
from jax.experimental.pallas import tpu as pltpu
from jax.sharding import PartitionSpec as P

BX = 64
BY = 48
SB = 16
TILE = 256
CAP = 4
FEAT = 8
KEPT = 7
C1 = 256
C2 = 512
SUBS = 12
PHASES = 4
QUADS = BY // PHASES
ROW_LANES = PHASES * FEAT
FAR = 8192.0
ROOT_HALF_LOG2E = (0.5 * 1.4426950408889634) ** 0.5
SOURCES = 128


def iota(shape, axis):
    return lax.broadcasted_iota(jnp.int32, shape, axis)


def setconv_kernel(note_ref, tiles_ref, out_ref, *sums):
    step = pl.program_id(0)

    @pl.when(step == 0)
    def _():
        for total in sums:
            total[...] = jnp.zeros_like(total)

    row = iota((SB, 1), 0)
    lane = iota((1, TILE), 1)
    center_row = (row.astype(jnp.float32) + 0.5) * ROOT_HALF_LOG2E
    center_col = ((row % 4 * 4 + row // 4).astype(jnp.float32) + 0.5) * ROOT_HALF_LOG2E

    def add_tile(source, slot, total):
        tile = jnp.concatenate([tiles_ref[source, slot], tiles_ref[source, slot + CAP]], axis=1)
        place = tile.astype(jnp.float32)
        live = lane < note_ref[step * SOURCES + source, CAP + slot]
        place_row = jnp.where(live, place[0:1], FAR)
        off_row = center_row - place_row * ROOT_HALF_LOG2E
        off_col = center_col - place[1:2] * ROOT_HALF_LOG2E
        along_row = jnp.exp2(-(off_row * off_row)).astype(jnp.bfloat16)
        along_col = jnp.exp2(-(off_col * off_col)).astype(jnp.bfloat16)
        weighted = [along_row]
        weighted += [tile[k : k + 1] * along_row for k in range(2, FEAT)]
        part = lax.dot_general(
            along_col,
            jnp.concatenate(weighted, axis=0),
            (((1,), (1,)), ((), ())),
            preferred_element_type=jnp.float32,
        )
        sub = note_ref[step * SOURCES + source, slot]
        total[sub] = total[sub] + part

    for k in range(SOURCES):
        for slot in range(CAP):
            add_tile(k, slot, sums[slot])

    @pl.when(step == pl.num_programs(0) - 1)
    def _():
        total = sums[0][...]
        for more in sums[1:]:
            total = total + more[...]
        total = total.reshape(SUBS * SB, KEPT * SB)
        total = jnp.concatenate([total, jnp.zeros((SUBS * SB, SB), jnp.float32)], axis=1)
        lane = iota((SUBS * SB, 128), 1)
        density = jnp.where(lane < SB, total, 0.0)
        for places in (SB, 2 * SB, 4 * SB):
            density = density + pltpu.roll(density, places, axis=1)
        grid = jnp.where(lane < SB, jnp.log1p(density), total / (1.0 + density))
        grid = grid.astype(jnp.bfloat16)
        target = iota((4 * SB, 1), 0)
        source = iota((1, SUBS * SB), 1)
        quad = target & (SB - 1)
        wanted = (target >> 4) * BY + (quad >> 2) * SB + (quad & 3)
        wanted = jnp.where(quad < QUADS, wanted, -SUBS * SB)
        parts = []
        for phase in range(PHASES):
            take = (source == wanted + 4 * phase).astype(jnp.bfloat16)
            parts.append(
                jnp.dot(take, grid, preferred_element_type=jnp.float32).astype(jnp.bfloat16)
            )
        spread = jnp.concatenate(parts, axis=1)
        lane_in = iota((512, 1), 0)
        lane_out = (lane_in & 15) * ROW_LANES + (lane_in >> 7) * FEAT + ((lane_in & 127) >> 4)
        moved = (iota((1, 512), 1) == lane_out).astype(jnp.bfloat16)
        ordered = jnp.dot(spread, moved, preferred_element_type=jnp.float32).astype(jnp.bfloat16)
        to = iota((8 * QUADS, 1), 0)
        block = to // QUADS
        quad = to - block * QUADS
        start = iota((1, 4 * SB), 1)
        for half in range(2):
            rows = None
            for k in range(4):
                wanted = (2 * half + (block >> 2)) * SB + quad
                take = start == jnp.where((block & 3) == k, wanted, -1)
                part = jnp.dot(
                    take.astype(jnp.bfloat16),
                    ordered[:, 128 * k : 128 * k + 128],
                    preferred_element_type=jnp.float32,
                )
                rows = part if rows is None else rows + part
            rows = rows.astype(jnp.bfloat16)
            for k in range(out_ref.shape[0] // 2):
                out_ref[2 * k + half] = rows


def set_convolution(notes, arrived, copies):
    out = jax.ShapeDtypeStruct((copies, 8 * QUADS, 128), jnp.bfloat16)
    return pl.pallas_call(
        setconv_kernel,
        grid_spec=pltpu.PrefetchScalarGridSpec(
            num_scalar_prefetch=1,
            grid=(arrived.shape[0] // SOURCES,),
            in_specs=[pl.BlockSpec((SOURCES,) + arrived.shape[1:], lambda i, *_: (i, 0, 0, 0))],
            out_specs=pl.BlockSpec(out.shape, lambda i, *_: (0, 0, 0)),
            scratch_shapes=[pltpu.VMEM((SUBS, SB, KEPT * SB), jnp.float32)] * CAP,
        ),
        out_shape=out,
        compiler_params=pltpu.CompilerParams(
            dimension_semantics=("arbitrary",), vmem_limit_bytes=24 << 20
        ),
    )(notes, arrived)


def leave_kernel(sub_ref, rows_ref, tiles_ref, out_ref, notes_ref):
    step = pl.program_id(0)
    count = tiles_ref.shape[0]

    @pl.when(step == 0)
    def _():
        both = jnp.concatenate([sub_ref[...], rows_ref[...]], axis=0).astype(jnp.float32)
        blank = jnp.zeros((128 - 2 * CAP, both.shape[1]), jnp.float32)
        notes_ref[...] = jnp.concatenate([both, blank], axis=0).T

    notes = notes_ref[pl.ds(step * count, count), :]
    notes = jnp.broadcast_to(notes[:, None, :], (count, FEAT, 128)).astype(jnp.bfloat16)
    out_ref[:, :CAP] = tiles_ref[:, :, :, :128]
    out_ref[:, CAP : 2 * CAP] = tiles_ref[:, :, :, 128:]
    out_ref[:, 2 * CAP] = notes


def leaving_tiles(tiles, subs, rows):
    count = tiles.shape[0]
    part = count // 2
    return pl.pallas_call(
        leave_kernel,
        grid=(2,),
        in_specs=[
            pl.BlockSpec(subs.shape, lambda i: (0, 0)),
            pl.BlockSpec(rows.shape, lambda i: (0, 0)),
            pl.BlockSpec((part,) + tiles.shape[1:], lambda i: (i, 0, 0, 0)),
        ],
        out_specs=pl.BlockSpec((part, 2 * CAP + 1, FEAT, 128), lambda i: (i, 0, 0, 0)),
        out_shape=jax.ShapeDtypeStruct((count, 2 * CAP + 1, FEAT, 128), jnp.bfloat16),
        scratch_shapes=[pltpu.VMEM((count, 128), jnp.float32)],
        compiler_params=pltpu.CompilerParams(vmem_limit_bytes=60 << 20),
    )(subs, rows, tiles)


def placed(params, count, above, shift, low, high):
    lane = iota((count, params.shape[0]), 0)
    row_tap = lane // ROW_LANES - above
    col_tap = lane // FEAT % PHASES + shift
    wanted = (3 * row_tap + col_tap) * FEAT + lane % FEAT
    inside = (row_tap >= 0) & (row_tap < 3) & (col_tap >= low) & (col_tap < high)
    take = (inside & (iota(lane.shape, 1) == wanted)).astype(jnp.bfloat16)
    return jnp.dot(take, params, preferred_element_type=jnp.float32).astype(jnp.bfloat16)


def conv_kernel(first_block, *refs):
    flag_ref, *halo, own_ref, params_ref, weight2_hbm = refs[: 4 + (first_block == 0)]
    (out_ref, send_ref, wide_ref, grid_ref, moved_ref, even_rows, odd_rows, weight2_ref, odd1_ref,
     odd2_ref, even1_ref, even2_ref, rows_ref, sem, out_sem) = refs[-15:]
    bias1 = params_ref[9 * FEAT : 9 * FEAT + 1, :]
    bias2 = jnp.concatenate(
        [params_ref[9 * FEAT + 1 : 9 * FEAT + 2, :], params_ref[9 * FEAT + 2 : 9 * FEAT + 3, :]],
        axis=1,
    )
    columns = grid_ref.shape[0]
    loads = [
        pltpu.make_async_copy(
            weight2_hbm.at[tap, pl.ds(C1 * k, C1)], weight2_ref.at[tap, pl.ds(C1 * k, C1)], sem.at[tap, k]
        )
        for tap in range(3)
        for k in range(3)
    ]

    def first_row(t):
        block = t // 2
        if t % 2 == 0:
            here = grid_ref[:, 128 * block : 128 * block + 128]
            left = moved_ref[:, 128 * block : 128 * block + 128]
            odd = jnp.dot(here, odd1_ref[...], preferred_element_type=jnp.float32)
            weights = even1_ref
        else:
            here = grid_ref[:, 128 * block : 128 * block + 256]
            left = moved_ref[:, 128 * block : 128 * block + 256]
            odd = jnp.dot(here, odd2_ref[...], preferred_element_type=jnp.float32)
            weights = even2_ref
        even = jnp.dot(
            jnp.concatenate([here, left], axis=1), weights[...], preferred_element_type=jnp.float32
        )

        def activate(half):
            half = half + bias1
            return half * jnp.tanh(half) + half

        odd = activate(odd)
        even = activate(even)
        if t == 0:
            live = flag_ref[1].astype(jnp.float32)
            odd = odd * live
            even = even * live
        before = pltpu.roll(odd, 1, axis=0)
        store = even_rows if t % 2 == 0 else odd_rows
        at = pl.ds(block * columns, columns)
        store[at, 0:C1] = odd.astype(jnp.bfloat16)
        store[at, C1 : 2 * C1] = even.astype(jnp.bfloat16)
        store[at, 2 * C1 :] = before.astype(jnp.bfloat16)

    def second_row(row):
        total = None
        for tap, (store, at) in enumerate(
            [(even_rows, row), (odd_rows, row), (even_rows, row + 1)]
        ):
            part = jnp.dot(
                store[at * columns : (at + 1) * columns, :],
                weight2_ref[tap],
                preferred_element_type=jnp.float32,
            )
            total = part if total is None else total + part
        if row >= 2:
            for store in stores(row - 2):
                store.wait()
        rows_ref[row % 2] = (total + bias2).astype(jnp.bfloat16)
        for store in stores(row):
            store.start()

    def stores(row):
        out_row = flag_ref[0] * 8 + first_block + row
        half = columns // 2
        return [
            pltpu.make_async_copy(
                rows_ref.at[row % 2, pl.ds(half * k, half)],
                target.at[at, pl.ds(half * k, half)],
                out_sem.at[row % 2, side, k],
            )
            for side, (target, at) in enumerate([(out_ref, out_row), (send_ref, row)])
            for k in range(2)
        ]

    for load in loads:
        load.start()
    params = params_ref[...].astype(jnp.bfloat16)
    odd1_ref[...] = placed(params, 128, 1, -1, 0, 3)
    odd2_ref[...] = placed(params, 256, 3, -1, 0, 3)
    even1_ref[0:128, :] = placed(params, 128, 1, 1, 1, 3)
    even1_ref[128:256, :] = placed(params, 128, 1, -3, 0, 1)
    even2_ref[0:256, :] = placed(params, 256, 3, 1, 1, 3)
    even2_ref[256:512, :] = placed(params, 256, 3, -3, 0, 1)
    for source in range(own_ref.shape[0]):
        own = own_ref[source].astype(jnp.float32)
        parts = [own[QUADS * k : QUADS * (k + 1)] for k in range(first_block, first_block + 4)]
        if first_block == 0:
            parts = [halo[0][source].astype(jnp.float32)[SB - QUADS :]] + parts
        else:
            parts = [own[QUADS * (first_block - 1) : QUADS * first_block]] + parts
        for k, part in enumerate(parts):
            wide_ref[QUADS * source : QUADS * (source + 1), 128 * k : 128 * (k + 1)] = part
    grid_ref[...] = wide_ref[...].astype(jnp.bfloat16)
    moved_ref[...] = pltpu.roll(wide_ref[...], 1, axis=0).astype(jnp.bfloat16)
    for t in range(3):
        first_row(t)
    for load in loads:
        load.wait()
    second_row(0)

    for row in range(1, 4):
        first_row(2 * row + 1)
        first_row(2 * row + 2)
        second_row(row)
    for store in stores(2) + stores(3):
        store.wait()


def convolutions(part, flags, halo, own, params, weights2, whole):
    columns = QUADS * own.shape[0]
    full = lambda a: pl.BlockSpec(a.shape, lambda i, *_: (0,) * a.ndim)
    anywhere = pl.BlockSpec(memory_space=pl.ANY)
    operands = [own, params, weights2]
    if part == 0:
        operands = [halo] + operands
    specs = [anywhere if a is weights2 else full(a) for a in operands]
    aliases = {}
    if whole is not None:
        aliases = {1 + len(operands): 0}
        operands.append(whole)
        specs.append(anywhere)
    return pl.pallas_call(
        functools.partial(conv_kernel, 4 * part),
        grid_spec=pltpu.PrefetchScalarGridSpec(
            num_scalar_prefetch=1,
            grid=(1,),
            in_specs=specs,
            out_specs=[anywhere, anywhere],
            scratch_shapes=[
                pltpu.VMEM((columns, 640), jnp.float32),
                pltpu.VMEM((columns, 640), jnp.bfloat16),
                pltpu.VMEM((columns, 640), jnp.bfloat16),
                pltpu.VMEM((5 * columns, 3 * C1), jnp.bfloat16),
                pltpu.VMEM((4 * columns, 3 * C1), jnp.bfloat16),
                pltpu.VMEM(weights2.shape, jnp.bfloat16),
                pltpu.VMEM((128, C1), jnp.bfloat16),
                pltpu.VMEM((256, C1), jnp.bfloat16),
                pltpu.VMEM((256, C1), jnp.bfloat16),
                pltpu.VMEM((512, C1), jnp.bfloat16),
                pltpu.VMEM((2, columns, C2), jnp.bfloat16),
                pltpu.SemaphoreType.DMA((3, 3)),
                pltpu.SemaphoreType.DMA((2, 2, 2)),
            ],
        ),
        out_shape=[
            jax.ShapeDtypeStruct((16, columns, C2), jnp.bfloat16),
            jax.ShapeDtypeStruct((4, columns, C2), jnp.bfloat16),
        ],
        input_output_aliases=aliases,
        cost_estimate=pl.CostEstimate(
            flops=9_000_000_000, transcendentals=1_800_000, bytes_accessed=12_000_000
        ),
        compiler_params=pltpu.CompilerParams(
            dimension_semantics=("arbitrary",), vmem_limit_bytes=(40 if part else 40) << 20
        ),
    )(flags, *operands)


def first_weights(embed_weight, conv1_weight):
    channels = conv1_weight.astype(jnp.float32)
    values = jnp.einsum(
        "vc,tco->tvo",
        embed_weight.astype(jnp.float32),
        channels[:, 1:],
        precision=lax.Precision.HIGHEST,
    )
    taps = jnp.concatenate([channels[:, :1], values, jnp.zeros_like(channels[:, :1])], axis=1)
    return 0.5 * taps.reshape(9 * FEAT, C1)


def shards(
    obs_tiles,
    tile_block,
    tile_rows,
    embed_weight,
    conv1_weight,
    conv1_bias,
    conv2_weight,
    conv2_bias,
):
    n_lon = lax.axis_size("lon")
    n_lat = lax.axis_size("lat")
    core = lax.axis_index("lon") % 2

    leaving = leaving_tiles(obs_tiles[0], tile_block[0].T, tile_rows[0].T)
    arrived = lax.all_to_all(leaving, ("lat", "lon"), 0, 0, tiled=True)
    notes = arrived[:, 2 * CAP, 0, : 2 * CAP].astype(jnp.int32)

    halves = set_convolution(notes, arrived, n_lon)
    halves, conv2_weight = lax.optimization_barrier((halves, conv2_weight))
    own = lax.all_to_all(halves, "lon", 0, 0, tiled=True)
    last = own[:, 8 * QUADS - SB :]
    south = [(z * n_lon + i, z * n_lon + i + 1) for z in range(n_lat) for i in range(0, n_lon, 2)]
    south += [(b, b + n_lon - 1) for _, b in south if b + n_lon < n_lat * n_lon]
    halo = lax.ppermute(last, ("lat", "lon"), south)

    params = jnp.concatenate(
        [
            first_weights(embed_weight, conv1_weight),
            0.5 * conv1_bias[None],
            conv2_bias.reshape(2, C1),
            jnp.zeros((5, C1), jnp.float32),
        ],
        axis=0,
    )
    weights2 = conv2_weight.reshape(3, 3, C1, C2)[:, ::-1].reshape(3, 3 * C1, C2)
    top = jnp.where((lax.axis_index("lat") == 0) & (core == 0), 0, 1)
    pairs = [(i, i ^ 1) for i in range(n_lon)]
    whole = None
    swapped = []
    for part in (1, 0):
        flags = jnp.stack([core, top if part == 0 else jnp.ones_like(top)]).astype(jnp.int32)
        whole, half = convolutions(
            part,
            flags,
            halo,
            own,
            params,
            weights2,
            whole,
        )
        swapped.append((part, lax.ppermute(half, "lon", pairs)))
    for part, rows in swapped:
        whole = lax.dynamic_update_slice_in_dim(whole, rows, (1 - core) * 8 + 4 * part, axis=0)
    return whole


def solution(mesh):
    placed = (
        P(("lat", "lon"), None, None, None, None),
        P(("lat", "lon"), None, None),
        P(("lat", "lon"), None, None),
        P(),
        P(),
        P(),
        P(),
        P(),
    )
    return jax.shard_map(
        shards, mesh=mesh, in_specs=placed, out_specs=P("lat", None, None), check_vma=False
    )
```
